256 devices in a mesh: dp: 32 (over y, z), mp: 8 (over x, core).
Axes of the slice: x: 4, y: 4, z: 8, core: 2. Of those that a mesh axis runs over, the one named last changes fastest.
Arguments:
- tokens: bfloat16 [8192, 2048], P('dp'), may hold values from -6 to 6
- out_grad: bfloat16 [8192, 2048], P('dp'), may hold values from -6 to 6
- master: float32 [2240, 3, 7168], P('dp', None, 'mp'), may hold values from -6 to 6
- moment_one: float32 [2240, 3, 7168], P('dp', None, 'mp'), may hold values from -6 to 6
- moment_two: float32 [2240, 3, 7168], P('dp', None, 'mp'), may hold values from 0.05 to 5
- old_offsets: int32 [33], replicated, may hold values from 0 to 2048, as said below
- new_offsets: int32 [33], replicated, may hold values from 0 to 2048, as said below
Outputs:
- new_master: float32 [2752, 3, 7168], P('dp', None, 'mp')
- new_moment_one: float32 [2752, 3, 7168], P('dp', None, 'mp')
- new_moment_two: float32 [2752, 3, 7168], P('dp', None, 'mp')
- layer_output: bfloat16 [8192, 2048], P('dp', 'mp')
The draws below stay inside these ranges and needn't reach their ends.
Inputs may be any that keep to these rules, and one draw needn't show every extreme that they name: non-decreasing, old_offsets[0] = 0 and old_offsets[32] = 2048; device p holds rows old_offsets[p] to old_offsets[p + 1] - 1 in its first slots; every device holds at least one and at most 70 rows, and some device exactly 70. non-decreasing, new_offsets[0] = 0 and new_offsets[32] = 2048; exactly one device holds no rows, its index at least 2 and at most 15; every other device holds at least one and at most 86 rows, some device exactly 86; a row's device in the new layout is its device in the old layout or the next one along dp.
All inputs are finite; a program needn't handle non-finite values.
Results may differ from the reference program's by a relative error of at most 0.014.
Values may be sent and summed in bfloat16 or wider, within the bound.
No kernel may reach another device: no remote copies, remote signals or barrier semaphores. Data moves between devices by JAX's collectives and lax.ppermute only.
A program may use at most 128 MiB of HBM per device.

```python
import math
import jax
import jax.numpy as jnp
from jax import lax

FEATURE_WIDTH = 2048
FF = 7168
TOK_DEV = 256
TOKENS = 8192
SHARD = 64
MAX_SHIFT = 3
CAP_OLD = 70
CAP_NEW = 86
N_DP = 32
N_MP = 8


def full_layout(key):
    base_key = jax.random.fold_in(key, 11)
    lost_key, forced_key, wiggle_key = jax.random.split(base_key, 3)
    leaving = jax.random.randint(lost_key, (), 2, N_DP // 2, dtype=jnp.int32)
    forced = jax.random.randint(forced_key, (), 2, N_DP - 2, dtype=jnp.int32)
    device_ids = jnp.arange(N_DP + 1, dtype=jnp.int32)
    wiggle = jax.random.randint(wiggle_key, (N_DP + 1,), -1, 2, dtype=jnp.int32)
    free_bound = (device_ids > 0) & (device_ids < N_DP) & (device_ids != forced) & (device_ids != forced + 1)
    old_bounds = device_ids * SHARD
    old_bounds = old_bounds + jnp.where(device_ids == forced, -MAX_SHIFT, 0)
    old_bounds = old_bounds + jnp.where(device_ids == forced + 1, MAX_SHIFT, 0)
    old_bounds = (old_bounds + jnp.where(free_bound, wiggle, 0)).astype(jnp.int32)
    old_sizes = (old_bounds[1:] - old_bounds[:-1]).astype(jnp.int32)
    lost_size = jnp.sum(jnp.where(jnp.arange(N_DP, dtype=jnp.int32) == leaving, old_sizes, 0)).astype(jnp.int32)

    def carry_step(previous, inputs):
        position, size_before = inputs
        pushed = jnp.maximum(previous + size_before - CAP_NEW, 1)
        moved_rows = jnp.where(position < leaving, 1, jnp.where(position == leaving, 0, jnp.where(position == leaving + 1, lost_size, pushed))).astype(jnp.int32)
        return (moved_rows, moved_rows)
    final_moved, inner_moves = lax.scan(carry_step, jnp.zeros((), jnp.int32), (jnp.arange(1, N_DP, dtype=jnp.int32), old_sizes[:-1]))
    boundary_moves = jnp.concatenate([jnp.zeros((1,), jnp.int32), inner_moves, jnp.zeros((1,), jnp.int32)])
    new_bounds = (old_bounds - boundary_moves).astype(jnp.int32)
    return (old_bounds, new_bounds)


def draw_new_offsets(key, part):
    old_bounds, new_bounds = full_layout(key)
    return new_bounds


def draw_old_offsets(key, part):
    old_bounds, new_bounds = full_layout(key)
    return old_bounds


def spiked(values, stream_key, source, target, blocks, factor):
    def block_of(dim):
        return (jnp.arange(values.shape[dim]) // (values.shape[dim] // blocks)).reshape((-1,) + (1,) * (values.ndim - 1 - dim))

    first = jax.random.permutation(stream_key, blocks)[block_of(target)]
    other_side = (block_of(target) + blocks // 2) % blocks
    return jnp.where((block_of(source) == first) | (block_of(source) == other_side), factor * values, values)


def level_of(own_key, shape, cuts, low, high):
    factor_of, own = 1.0, jax.random.fold_in(own_key, 6)
    for axis_at, parts in cuts:
        steps = jnp.exp(jax.random.uniform(jax.random.fold_in(own, axis_at), (parts,), jnp.float32, low / len(cuts), high / len(cuts)))
        factor_of = factor_of * jnp.repeat(steps, shape[axis_at] // parts).reshape([-1 if axis == axis_at else 1 for axis in range(len(shape))])
    return factor_of


def normal_values(key, shape, width, bound, pieces=(), kind=jnp.bfloat16):
    loudness = level_of(key, shape, pieces, -0.22, 0.18) if pieces else 1.0
    values = jax.random.normal(key, shape, jnp.float32) * width * loudness
    return jnp.minimum(jnp.maximum(values, -bound), bound).astype(kind)


def noise_with(own_key, shape, scale, limit, cuts, heavy, kind=jnp.bfloat16):
    entries = scale * jax.random.normal(own_key, shape, jnp.float32)
    if cuts:
        entries = entries * level_of(own_key, shape, cuts, -0.22, 0.18)
    return jnp.clip(spiked(entries, jax.random.fold_in(own_key, 3), *heavy), -limit, limit).astype(kind)


def setup_inputs(seed: int = 0) -> dict:
    splits = jax.random.split(jax.random.key(seed), 8)
    tokens = noise_with(splits[0], (TOKENS, FEATURE_WIDTH), 1.0, 6.0, ((0, 32),), (0, 1, 32, 2.75))
    out_grad = normal_values(splits[1], (TOKENS, FEATURE_WIDTH), 1.0, 6.0, ((0, 32),))
    master = normal_values(splits[2], (N_DP * CAP_OLD, 3, FF), 1.0, 6.0, ((0, 32), (2, 8)), jnp.float32)
    moment_one = normal_values(splits[3], (N_DP * CAP_OLD, 3, FF), 1.0, 6.0, ((0, 32), (2, 8)), jnp.float32)
    moment_two = jnp.clip(jnp.exp(math.log(5.0) - 4.6051702 * jax.random.uniform(splits[4], (N_DP * CAP_OLD, 3, FF), jnp.float32) ** level_of(splits[4], (N_DP * CAP_OLD, 3, FF), ((0, 32), (2, 8)), -0.2, 0.2)), 0.05, 5.0)
    old_offsets = draw_old_offsets(jax.random.fold_in(splits[7], 71), 0)
    new_offsets = draw_new_offsets(jax.random.fold_in(splits[7], 71), 0)
    return dict(tokens=tokens, out_grad=out_grad, master=master, moment_one=moment_one, moment_two=moment_two, old_offsets=old_offsets, new_offsets=new_offsets)


beta_one = 0.9
beta_two = 0.95
learn_rate = 0.01
decay_rate = 0.1
adam_eps = 1e-08
bias_one = 1.0 - 0.9 ** 10
bias_two = 1.0 - 0.95 ** 10

def lookup(small_table, wanted):
    matches = wanted[..., None] == jnp.arange(small_table.shape[0], dtype=jnp.int32)
    return lax.optimization_barrier(jnp.sum(jnp.where(matches, small_table, 0), axis=-1)).astype(jnp.int32)

def unpack(packed, offsets, capacity):
    row_index = jnp.arange(FEATURE_WIDTH, dtype=jnp.int32)
    owner_index = lax.optimization_barrier(jnp.sum((offsets[1:N_DP][None, :] <= row_index[:, None]).astype(jnp.int32), axis=1)).astype(jnp.int32)
    slot_index = owner_index * capacity + row_index - lookup(offsets, owner_index)
    return jnp.take(packed, slot_index.astype(jnp.int32), axis=0)

def pack(full_rows, offsets, capacity):
    slot_index = jnp.arange(N_DP * capacity, dtype=jnp.int32)
    owner_index = slot_index // capacity
    local_index = slot_index - owner_index * capacity
    row_start = lookup(offsets, owner_index)
    in_range = local_index < lookup(offsets, owner_index + 1) - row_start
    row_index = jnp.clip(row_start + local_index, 0, FEATURE_WIDTH - 1).astype(jnp.int32)
    picked = jnp.take(full_rows, row_index, axis=0)
    return jnp.where(in_range[:, None, None, None], picked, 0.0)

def adam_step(master_rows, first_rows, second_rows, grads):
    first_new = beta_one * first_rows + (1.0 - beta_one) * grads
    second_new = beta_two * second_rows + (1.0 - beta_two) * grads * grads
    update = first_new / bias_one / (jnp.sqrt(second_new / bias_two) + adam_eps)
    master_new = master_rows - learn_rate * (update + decay_rate * master_rows)
    return (master_new, first_new, second_new)

def reference(tokens, out_grad, master, moment_one, moment_two, old_offsets, new_offsets):
    full_rows = unpack(jnp.stack([master, moment_one, moment_two], axis=1), old_offsets, CAP_OLD)
    weights = full_rows[:, 0].astype(jnp.bfloat16)
    gate_weight = weights[:, 0]
    up_weight = weights[:, 1]
    down_weight = weights[:, 2]
    scale_in = FEATURE_WIDTH ** (-0.5)
    scale_hidden = FF ** (-0.5)
    block_width = FF // N_MP
    down_blocks = down_weight.astype(jnp.float32).reshape(FEATURE_WIDTH, N_MP, block_width)
    live_flags = new_offsets[1:] != new_offsets[:-1]

    def one_group(grad_total, inputs):
        group_tokens, group_upstream, live_flag = inputs
        upstream = jnp.where(live_flag, group_upstream, jnp.zeros_like(group_upstream))
        gate_act = jnp.dot(group_tokens, gate_weight, preferred_element_type=jnp.float32) * scale_in
        up_act = jnp.dot(group_tokens, up_weight, preferred_element_type=jnp.float32) * scale_in
        sigmoid_gate = jax.nn.sigmoid(gate_act)
        hidden = (gate_act * sigmoid_gate * up_act).astype(jnp.bfloat16)
        hidden_blocks = hidden.astype(jnp.float32).reshape(TOK_DEV, N_MP, block_width)
        partial_value = jnp.einsum('tcf,dcf->ctd', hidden_blocks, down_blocks, precision=lax.Precision.HIGHEST) * scale_hidden
        partial_value = jnp.where(live_flag, partial_value, 0.0).astype(jnp.bfloat16)
        group_output = lax.optimization_barrier(jnp.sum(lax.optimization_barrier(partial_value).astype(jnp.float32), axis=0)).astype(jnp.bfloat16)
        back_grad = jnp.dot(upstream, down_weight, preferred_element_type=jnp.float32) * scale_hidden
        gate_grad = (back_grad * up_act * sigmoid_gate * (1.0 + gate_act * (1.0 - sigmoid_gate))).astype(jnp.bfloat16)
        up_grad = (back_grad * gate_act * sigmoid_gate).astype(jnp.bfloat16)
        term_rows = jnp.stack([jnp.dot(group_tokens.T, gate_grad, preferred_element_type=jnp.float32) * scale_in, jnp.dot(group_tokens.T, up_grad, preferred_element_type=jnp.float32) * scale_in, jnp.dot(upstream.T, hidden, preferred_element_type=jnp.float32) * scale_hidden], axis=1)
        rounded = lax.optimization_barrier(term_rows.astype(jnp.bfloat16)).astype(jnp.float32)
        return (grad_total + rounded, group_output)
    grad_total, outputs = lax.scan(one_group, jnp.zeros((FEATURE_WIDTH, 3, FF), jnp.float32), (tokens.reshape(N_DP, TOK_DEV, FEATURE_WIDTH), out_grad.reshape(N_DP, TOK_DEV, FEATURE_WIDTH), live_flags))
    new_rows = jnp.stack(adam_step(full_rows[:, 0], full_rows[:, 1], full_rows[:, 2], grad_total), axis=1)
    packed = pack(new_rows, new_offsets, CAP_NEW)
    return (packed[:, 0], packed[:, 1], packed[:, 2], outputs.reshape(TOKENS, FEATURE_WIDTH))
```

```python
import jax
import jax.numpy as jnp
from jax import lax
from jax.sharding import Mesh, PartitionSpec as P

FEATURE_WIDTH = 2048
FF = 7168
NY, NZ, NX, NCORE = 4, 8, 4, 2
ROWS = 64
CAP_OLD = 70
CAP_NEW = 86
COLS = 896
QUART = COLS // NY
WIDE = 256
EDGE = 8

beta_one = 0.9
beta_two = 0.95
learn_rate = 0.01
decay_rate = 0.1
adam_eps = 1e-08
bias_one = 1.0 - 0.9**10
bias_two = 1.0 - 0.95**10

bf16 = jnp.bfloat16
f32 = jnp.float32
DP = ("y", "z")
MP = ("x", "core")


def ring(value, axis, by, size):
    return lax.ppermute(value, axis, [(i, (i + by) % size) for i in range(size)])


def along_dp(value, by):
    peers = NY * NZ
    pairs = [(i, i + by) for i in range(peers) if 0 <= i + by < peers]
    return lax.ppermute(value, DP, pairs)


def rows_from(value, start, count, front, back):
    padding = [(front, back)] + [(0, 0)] * (value.ndim - 1)
    return lax.dynamic_slice_in_dim(jnp.pad(value, padding), front + start, count, axis=0)


def row_mask(condition):
    return condition[:, None, None]


def adam_step(master_rows, first_rows, second_rows, grads):
    first_new = beta_one * first_rows + (1.0 - beta_one) * grads
    second_new = beta_two * second_rows + (1.0 - beta_two) * grads * grads
    update = first_new / bias_one / (jnp.sqrt(second_new / bias_two) + adam_eps)
    master_new = master_rows - learn_rate * (update + decay_rate * master_rows)
    return (master_new, first_new, second_new)


def even_rows(master, old_start, old_end, p):
    own = master.astype(bf16)
    shift = old_start - ROWS * p
    over = old_end - ROWS * (p + 1)
    rows = jnp.arange(ROWS, dtype=jnp.int32)
    tail = along_dp(rows_from(own, ROWS - shift, EDGE, 16, 16), 1)
    head = along_dp(rows_from(own, -shift - EDGE, EDGE, 16, 16), -1)
    even = rows_from(own, -shift, ROWS, 16, 16)
    first = jnp.where(row_mask(rows[:EDGE] < shift), tail, even[:EDGE])
    last = jnp.where(row_mask(rows[-EDGE:] >= ROWS + over), head, even[-EDGE:])
    return jnp.concatenate([first, even[EDGE:-EDGE], last], axis=0)


def gather_weights(even, z):
    split = even.reshape(ROWS, 3, NY, QUART)
    split = jnp.pad(split, ((0, 0), (0, 0), (0, 0), (0, WIDE - QUART)))
    split = jnp.transpose(split, (2, 0, 1, 3)).reshape(NY, ROWS, 3 * WIDE)
    own = lax.all_to_all(split, "y", split_axis=0, concat_axis=0, tiled=True)
    blocks = {0: own}
    right, left = own, own
    for step in range(1, NZ // 2):
        right = ring(right, "z", 1, NZ)
        left = ring(left, "z", -1, NZ)
        blocks[-step] = right
        blocks[step] = left
    half = NY // 2
    far_low = ring(right[:half], "z", 1, NZ)
    far_high = ring(left[half:], "z", -1, NZ)
    blocks[NZ // 2] = jnp.concatenate([far_low, far_high], axis=0)
    full = jnp.zeros((NY, NZ, ROWS, 3 * WIDE), bf16)
    for step, block in blocks.items():
        full = lax.dynamic_update_slice_in_dim(full, block[:, None], (z + step) % NZ, axis=1)
    return full.reshape(FEATURE_WIDTH, 3 * WIDE)


def gather_tokens(tokens, upstream, core):
    count = tokens.shape[0] // 2
    mine = jnp.stack(
        [lax.dynamic_slice_in_dim(v, core * count, count, axis=0) for v in (tokens, upstream)]
    )
    right = ring(mine, "y", 1, NY)
    left = ring(mine, "y", -1, NY)
    half = count // 2
    far = jnp.concatenate(
        [ring(right[:, :half], "y", 1, NY), ring(left[:, half:], "y", -1, NY)], axis=1
    )
    groups = jnp.stack([left, far, right])
    other = ring(groups, "core", 1, NCORE)
    first = jnp.where(core == 0, groups, other)
    second = jnp.where(core == 0, other, groups)
    both = jnp.concatenate([first, second], axis=2)
    return tuple(
        jnp.concatenate([v, both[0, i], both[1, i], both[2, i]], axis=0)
        for i, v in enumerate((tokens, upstream))
    )


def scatter_grads(terms, z):
    terms = terms.reshape(NY, NZ, ROWS, 3 * WIDE)

    def block(step):
        return lax.dynamic_slice_in_dim(terms, (z + step) % NZ, 1, axis=1)[:, 0]

    half = NY // 2

    def plus(a, b):
        return (a.astype(f32) + b.astype(f32)).astype(bf16)

    far = block(NZ // 2)
    right = ring(far[:half], "z", 1, NZ)
    left = ring(far[half:], "z", -1, NZ)
    up, down = block(NZ // 2 - 1), block(1 - NZ // 2)
    up = jnp.concatenate([plus(up[:half], right), up[half:]], axis=0)
    down = jnp.concatenate([down[:half], plus(down[half:], left)], axis=0)
    for step in range(NZ // 2 - 2, 0, -1):
        up = plus(block(step), ring(up, "z", 1, NZ))
        down = plus(block(-step), ring(down, "z", -1, NZ))
    up, down = ring(up, "z", 1, NZ), ring(down, "z", -1, NZ)
    return (block(0).astype(f32) + up.astype(f32) + down.astype(f32)).astype(bf16)


def new_rows_of_grads(grads, new_start, p):
    block = along_dp(grads, 1)
    before = along_dp(grads[-EDGE:], 2)
    after = along_dp(grads[:EDGE], -1)
    window = jnp.concatenate([before, block, grads, after], axis=0)
    return rows_from(window, new_start - (ROWS * (p - 1) - EDGE), CAP_NEW, 0, 32)


def body(tokens, out_grad, master, moment_one, moment_two, old_offsets, new_offsets):
    y, z, core = lax.axis_index("y"), lax.axis_index("z"), lax.axis_index("core")
    p = y * NZ + z
    old_start, old_end = old_offsets[p], old_offsets[p + 1]
    old_before = old_offsets[jnp.maximum(p - 1, 0)]
    new_start, new_end = new_offsets[p], new_offsets[p + 1]
    live = new_start != new_end
    scale_in = FEATURE_WIDTH ** (-0.5)
    scale_hidden = FF ** (-0.5)

    upstream = jnp.where(live, out_grad, jnp.zeros_like(out_grad))
    even = even_rows(master, old_start, old_end, p)
    weights = gather_weights(even, z)
    tokens_all, upstream_all = gather_tokens(tokens, upstream, core)

    states = (master, moment_one, moment_two)
    from_left = along_dp(jnp.stack(states).astype(bf16), 1)

    def dot(a, b, contract=(1, 0)):
        return lax.dot_general(
            a, b, (((contract[0],), (contract[1],)), ((), ())), preferred_element_type=f32
        )

    gate_up = dot(tokens_all, weights[:, : 2 * WIDE]) * scale_in
    gate, up = gate_up[:, :WIDE], gate_up[:, WIDE:]
    down_weight = weights[:, 2 * WIDE :]
    back = dot(upstream_all, down_weight) * scale_hidden
    sigmoid = jax.nn.sigmoid(gate)
    hidden = (gate * sigmoid * up).astype(bf16)
    gate_grad = (back * up * sigmoid * (1.0 + gate * (1.0 - sigmoid))).astype(bf16)
    up_grad = (back * gate * sigmoid).astype(bf16)
    partial = (dot(hidden, down_weight, (1, 1)) * scale_hidden).astype(bf16)
    terms = jnp.concatenate(
        [
            (dot(tokens_all, jnp.concatenate([gate_grad, up_grad], axis=1), (0, 0)) * scale_in).astype(bf16),
            (dot(upstream_all, hidden, (0, 0)) * scale_hidden).astype(bf16),
        ],
        axis=1,
    )

    shared = lax.psum_scatter(partial, MP, scatter_dimension=1, tiled=True)
    shared = shared.reshape(NY, tokens.shape[0], -1)
    total = shared[0].astype(f32)
    for step in range(1, NY):
        total = total + ring(shared[step], "y", step, NY).astype(f32)
    layer_output = jnp.where(live, total, 0.0).astype(bf16)

    summed = scatter_grads(terms, z)
    quarters = lax.all_to_all(summed, "y", split_axis=0, concat_axis=0, tiled=True)
    quarters = quarters.reshape(NY, ROWS, 3, WIDE)[..., :QUART]
    grads = jnp.transpose(quarters, (1, 2, 0, 3)).reshape(ROWS, 3, COLS)
    grads = new_rows_of_grads(grads, new_start, p).astype(f32)

    slots = jnp.arange(CAP_NEW, dtype=jnp.int32)
    row = new_start + slots
    held = []
    for k, own in enumerate(states):
        moved = rows_from(from_left[k], new_start - old_before, CAP_NEW, 0, CAP_NEW).astype(f32)
        kept = rows_from(own, new_start - old_start, CAP_NEW, 72, 16)
        held.append(jnp.where(row_mask(row < old_start), moved, kept))
    updated = adam_step(*held, grads)
    in_range = row_mask(row < new_end)
    return tuple(jnp.where(in_range, v, 0.0) for v in updated) + (layer_output,)


def solution(mesh):
    grid = Mesh(mesh.devices.reshape(NY, NZ, NX, NCORE), DP + MP)
    state = P(DP, None, MP)
    return jax.shard_map(
        body,
        mesh=grid,
        in_specs=(P(DP, None), P(DP, None), state, state, state, P(), P()),
        out_specs=(state, state, state, P(DP, MP)),
        check_vma=False,
    )
```

```python
import jax
import jax.numpy as jnp
from jax import lax
from jax.sharding import Mesh, PartitionSpec as P

FEATURE_WIDTH = 2048
FF = 7168
NY, NZ, NX, NCORE = 4, 8, 4, 2
ROWS = 64
CAP_OLD = 70
CAP_NEW = 86
COLS = 896
QUART = COLS // NY
WIDE = 256
EDGE = 4
SENT = ROWS + 2 * EDGE

beta_one = 0.9
beta_two = 0.95
learn_rate = 0.01
decay_rate = 0.1
adam_eps = 1e-08
bias_one = 1.0 - 0.9**10
bias_two = 1.0 - 0.95**10

bf16 = jnp.bfloat16
f32 = jnp.float32
DP = ("y", "z")
MP = ("x", "core")


def ring(value, axis, by, size):
    return lax.ppermute(value, axis, [(i, (i + by) % size) for i in range(size)])


def wrapped(index, size):
    return lax.rem(index + size, jnp.int32(size))


def along_dp(value, by):
    peers = NY * NZ
    pairs = [(i, i + by) for i in range(peers) if 0 <= i + by < peers]
    return lax.ppermute(value, DP, pairs)


def rows_from(value, start, count, front, back):
    padding = [(front, back)] + [(0, 0)] * (value.ndim - 1)
    return lax.dynamic_slice_in_dim(jnp.pad(value, padding), front + start, count, axis=0)


def row_mask(condition):
    return condition[:, None, None]


def adam_step(master_rows, first_rows, second_rows, grads):
    first_new = beta_one * first_rows + (1.0 - beta_one) * grads
    second_new = beta_two * second_rows + (1.0 - beta_two) * grads * grads
    update = first_new / bias_one / (jnp.sqrt(second_new / bias_two) + adam_eps)
    master_new = master_rows - learn_rate * (update + decay_rate * master_rows)
    return (master_new, first_new, second_new)


def swap_along_y(pieces, y):
    def piece(step):
        return lax.dynamic_slice_in_dim(pieces, wrapped(y + step, NY), 1, axis=0)

    came = {step: ring(piece(step), "y", step, NY) for step in range(1, NY)}
    for step, value in came.items():
        pieces = lax.dynamic_update_slice_in_dim(pieces, value, wrapped(y - step, NY), axis=0)
    return pieces


def split_rows(master, shift, held):
    slots = jnp.arange(CAP_OLD, dtype=jnp.int32)
    own = jnp.where(row_mask(slots < held), master, 0.0).astype(bf16)
    rows = jnp.concatenate(
        [
            rows_from(own, -shift, ROWS, 16, 16),
            rows_from(own, -shift - EDGE, EDGE, 16, 16),
            rows_from(own, ROWS - shift, EDGE, 16, 16),
        ],
        axis=0,
    )
    split = rows.reshape(SENT, 3, NY, QUART)
    split = jnp.pad(split, ((0, 0), (0, 0), (0, 0), (0, WIDE - QUART)))
    return jnp.transpose(split, (2, 0, 1, 3)).reshape(NY, SENT, 3 * WIDE)


def gather_weights(own, beside):
    blocks = {0: own}
    right, left = own, own
    for step in range(1, NZ // 2):
        right = ring(right, "z", 1, NZ)
        left = ring(left, "z", -1, NZ)
        if step == 1:
            right, left, beside = lax.optimization_barrier((right, left, beside))
        blocks[-step] = right
        blocks[step] = left
    half = NY // 2
    far_low = ring(right[:half], "z", 1, NZ)
    far_high = ring(left[half:], "z", -1, NZ)
    blocks[NZ // 2] = jnp.concatenate([far_low, far_high], axis=0)
    return blocks, beside


def joined(blocks, z):
    full = jnp.zeros((NY, NZ, SENT, 3 * WIDE), bf16)
    for step, block in blocks.items():
        full = lax.dynamic_update_slice_in_dim(full, block[:, None], wrapped(z + step, NZ), axis=1)
    full = full.reshape(NY * NZ, SENT, 3 * WIDE)
    none = jnp.zeros((1, EDGE, 3 * WIDE), bf16)
    before = jnp.concatenate([full[1:, ROWS : ROWS + EDGE], none], axis=0)
    behind = jnp.concatenate([none, full[:-1, ROWS + EDGE :]], axis=0)
    main = full[:, :ROWS]
    main = jnp.concatenate(
        [main[:, :EDGE] + behind, main[:, EDGE:-EDGE], main[:, -EDGE:] + before], axis=1
    )
    return main.reshape(FEATURE_WIDTH, 3 * WIDE)


def after(values, others):
    return lax.optimization_barrier((values, others))[0]


def gather_tokens(tokens, upstream, core, blocks):
    count = tokens.shape[0] // 2
    mine = jnp.stack(
        [lax.dynamic_slice_in_dim(v, core * count, count, axis=0) for v in (tokens, upstream)]
    )
    right = ring(mine, "y", 1, NY)
    left = ring(mine, "y", -1, NY)
    right, left = after((right, left), (blocks[2], blocks[-2]))
    half = count // 2
    far = jnp.concatenate(
        [ring(right[:, :half], "y", 1, NY), ring(left[:, half:], "y", -1, NY)], axis=1
    )
    groups = after(jnp.stack([left, far, right]), (blocks[3], blocks[-3]))
    other = ring(groups, "core", 1, NCORE)
    first = jnp.where(core == 0, groups, other)
    second = jnp.where(core == 0, other, groups)
    both = jnp.concatenate([first, second], axis=2)
    return tuple(
        jnp.concatenate([v, both[0, i], both[1, i], both[2, i]], axis=0)
        for i, v in enumerate((tokens, upstream))
    )


def scatter_grads(terms, z):
    terms = terms.reshape(NY, NZ, ROWS, 3 * WIDE)

    def block(step):
        return lax.dynamic_slice_in_dim(terms, wrapped(z + step, NZ), 1, axis=1)[:, 0]

    half = NY // 2

    def plus(a, b):
        return (a.astype(f32) + b.astype(f32)).astype(bf16)

    far = block(NZ // 2)
    right = ring(far[:half], "z", 1, NZ)
    left = ring(far[half:], "z", -1, NZ)
    up, down = block(NZ // 2 - 1), block(1 - NZ // 2)
    up = jnp.concatenate([plus(up[:half], right), up[half:]], axis=0)
    down = jnp.concatenate([down[:half], plus(down[half:], left)], axis=0)
    for step in range(NZ // 2 - 2, 0, -1):
        up = plus(block(step), ring(up, "z", 1, NZ))
        down = plus(block(-step), ring(down, "z", -1, NZ))
    up, down = ring(up, "z", 1, NZ), ring(down, "z", -1, NZ)
    return (block(0).astype(f32) + up.astype(f32) + down.astype(f32)).astype(bf16)


def new_rows_of_grads(grads, new_start, p):
    block = along_dp(grads, 1)
    before = along_dp(grads[-EDGE:], 2)
    after = along_dp(grads[:EDGE], -1)
    window = jnp.concatenate([before, block, grads, after], axis=0)
    return rows_from(window, new_start - (ROWS * (p - 1) - EDGE), CAP_NEW, 0, 32)


def body(tokens, out_grad, master, moment_one, moment_two, old_offsets, new_offsets):
    y, z, core = lax.axis_index("y"), lax.axis_index("z"), lax.axis_index("core")
    p = y * NZ + z
    old_start = old_offsets[p]
    old_before = old_offsets[jnp.maximum(p - 1, 0)]
    new_start, new_end = new_offsets[p], new_offsets[p + 1]
    live = new_start != new_end
    scale_in = FEATURE_WIDTH ** (-0.5)
    scale_hidden = FF ** (-0.5)

    upstream = jnp.where(live, out_grad, jnp.zeros_like(out_grad))
    split = split_rows(master, old_start - ROWS * p, old_offsets[p + 1] - old_start)
    two_left = along_dp(jnp.stack([master, moment_one]).astype(bf16), 1)
    own = swap_along_y(split, y)
    tokens_in, upstream = after((tokens, upstream), own)
    blocks, two_left = gather_weights(own, two_left)
    tokens_all, upstream_all = gather_tokens(tokens_in, upstream, core, blocks)
    second_left = along_dp(after(moment_two, (blocks[3], blocks[-3])).astype(bf16), 1)
    weights = joined(blocks, z)
    states = (master, moment_one, moment_two)

    def dot(a, b, contract=(1, 0)):
        return lax.dot_general(
            a, b, (((contract[0],), (contract[1],)), ((), ())), preferred_element_type=f32
        )

    gate_up = dot(tokens_all, weights[:, : 2 * WIDE]) * scale_in
    gate, up = gate_up[:, :WIDE], gate_up[:, WIDE:]
    down_weight = weights[:, 2 * WIDE :]
    back = dot(upstream_all, down_weight) * scale_hidden
    sigmoid = jax.nn.sigmoid(gate)
    hidden = (gate * sigmoid * up).astype(bf16)
    gate_grad = (back * up * sigmoid * (1.0 + gate * (1.0 - sigmoid))).astype(bf16)
    up_grad = (back * gate * sigmoid).astype(bf16)
    hidden, second_left = lax.optimization_barrier((hidden, second_left))
    partial = (dot(hidden, down_weight, (1, 1)) * scale_hidden).astype(bf16)
    terms = jnp.concatenate(
        [
            (dot(tokens_all, jnp.concatenate([gate_grad, up_grad], axis=1), (0, 0)) * scale_in).astype(bf16),
            (dot(upstream_all, hidden, (0, 0)) * scale_hidden).astype(bf16),
        ],
        axis=1,
    )

    shared = lax.psum_scatter(partial, MP, scatter_dimension=1, tiled=True)
    shared = shared.reshape(NY, tokens.shape[0], -1)
    total = shared[0].astype(f32)
    for step in range(1, NY):
        total = total + ring(shared[step], "y", step, NY).astype(f32)
    layer_output = jnp.where(live, total, 0.0).astype(bf16)

    summed = scatter_grads(terms, z)
    from_left = (two_left[0], two_left[1], second_left)
    quarters = swap_along_y(summed, y)
    quarters = quarters.reshape(NY, ROWS, 3, WIDE)[..., :QUART]
    grads = jnp.transpose(quarters, (1, 2, 0, 3)).reshape(ROWS, 3, COLS)
    grads, layer_output = lax.optimization_barrier((grads, layer_output))
    grads = new_rows_of_grads(grads, new_start, p).astype(f32)

    slots = jnp.arange(CAP_NEW, dtype=jnp.int32)
    row = new_start + slots
    held = []
    for k, own in enumerate(states):
        moved = rows_from(from_left[k], new_start - old_before, CAP_NEW, 0, CAP_NEW).astype(f32)
        kept = rows_from(own, new_start - old_start, CAP_NEW, 72, 16)
        held.append(jnp.where(row_mask(row < old_start), moved, kept))
    updated = adam_step(*held, grads)
    in_range = row_mask(row < new_end)
    return tuple(jnp.where(in_range, v, 0.0) for v in updated) + (layer_output,)


def solution(mesh):
    grid = Mesh(mesh.devices.reshape(NY, NZ, NX, NCORE), DP + MP)
    state = P(DP, None, MP)
    return jax.shard_map(
        body,
        mesh=grid,
        in_specs=(P(DP, None), P(DP, None), state, state, state, P(), P()),
        out_specs=(state, state, state, P(DP, MP)),
        check_vma=False,
    )
```

```python
import jax
import jax.numpy as jnp
from jax import lax
from jax.sharding import Mesh, PartitionSpec as P

FEATURE_WIDTH = 2048
FF = 7168
NY, NZ, NX, NCORE = 4, 8, 4, 2
ROWS = 64
CAP_OLD = 70
CAP_NEW = 86
COLS = 896
QUART = COLS // NY
WIDE = 256
EDGE = 4
FIRST = 6
NEAR = 5
WIDTH = NY * ROWS
SENT = ROWS + 2 * EDGE

beta_one = 0.9
beta_two = 0.95
learn_rate = 0.01
decay_rate = 0.1
adam_eps = 1e-08
bias_one = 1.0 - 0.9**10
bias_two = 1.0 - 0.95**10

bf16 = jnp.bfloat16
f32 = jnp.float32
DP = ("y", "z")
MP = ("x", "core")


def ring(value, axis, by, size):
    return lax.ppermute(value, axis, [(i, (i + by) % size) for i in range(size)])


def wrapped(index, size):
    return lax.rem(index + size, jnp.int32(size))


def along_dp(value, by):
    peers = NY * NZ
    pairs = [(i, i + by) for i in range(peers) if 0 <= i + by < peers]
    return lax.ppermute(value, DP, pairs)


def rows_from(value, start, count, front, back):
    padding = [(front, back)] + [(0, 0)] * (value.ndim - 1)
    return lax.dynamic_slice_in_dim(jnp.pad(value, padding), front + start, count, axis=0)


def row_mask(condition):
    return condition[:, None, None]


def adam_step(master_rows, first_rows, second_rows, grads):
    first_new = beta_one * first_rows + (1.0 - beta_one) * grads
    second_new = beta_two * second_rows + (1.0 - beta_two) * grads * grads
    update = first_new / bias_one / (jnp.sqrt(second_new / bias_two) + adam_eps)
    master_new = master_rows - learn_rate * (update + decay_rate * master_rows)
    return (master_new, first_new, second_new)


def swap_along_y(pieces, y):
    def piece(step):
        return lax.dynamic_slice_in_dim(pieces, wrapped(y + step, NY), 1, axis=0)

    order = [piece(0)] + [ring(piece(step), "y", step, NY) for step in range(1, NY)]
    order = [order[0]] + order[:0:-1]
    return jnp.concatenate(
        [lax.select_n(wrapped(i - y, NY), *order) for i in range(NY)], axis=0
    )


def split_rows(master, shift, held):
    slots = jnp.arange(CAP_OLD, dtype=jnp.int32)
    own = jnp.where(row_mask(slots < held), master, 0.0).astype(bf16)
    rows = jnp.concatenate(
        [
            rows_from(own, -shift, ROWS, 16, 16),
            rows_from(own, -shift - EDGE, EDGE, 16, 16),
            rows_from(own, ROWS - shift, EDGE, 16, 16),
        ],
        axis=0,
    )
    split = rows.reshape(SENT, 3, NY, QUART)
    split = jnp.pad(split, ((0, 0), (0, 0), (0, 0), (0, WIDE - QUART)))
    return jnp.transpose(split, (2, 0, 1, 3)).reshape(NY, SENT, 3 * WIDE)


def gather_weights(own):
    blocks = {0: own}
    right, left = own, own
    for step in range(1, NZ // 2):
        right = ring(right, "z", 1, NZ)
        left = ring(left, "z", -1, NZ)
        blocks[NZ - step] = right
        blocks[step] = left
    half = NY // 2
    far_low = ring(right[:half], "z", 1, NZ)
    far_high = ring(left[half:], "z", -1, NZ)
    blocks[NZ // 2] = jnp.concatenate([far_low, far_high], axis=0)
    return blocks


def joined(blocks, chosen, z):
    none = jnp.zeros((1, EDGE, 3 * WIDE), bf16)
    parts = []
    for k in chosen:
        at = wrapped(z + k, NZ)
        behind = blocks[(k - 1) % NZ][:, ROWS + EDGE :]
        behind = jnp.where(at == 0, jnp.concatenate([none, behind[:-1]], axis=0), behind)
        ahead = blocks[(k + 1) % NZ][:, ROWS : ROWS + EDGE]
        ahead = jnp.where(at == NZ - 1, jnp.concatenate([ahead[1:], none], axis=0), ahead)
        main = blocks[k][:, :ROWS]
        behind = jnp.pad(behind, ((0, 0), (0, ROWS - EDGE), (0, 0)))
        ahead = jnp.pad(ahead, ((0, 0), (ROWS - EDGE, 0), (0, 0)))
        parts.append((main + behind + ahead).reshape(NY * ROWS, 3 * WIDE))
    return jnp.concatenate(parts, axis=0)


def ring_order(z):
    column = jnp.arange(FEATURE_WIDTH, dtype=jnp.int32)
    k, rest = column // (NY * ROWS), column % (NY * ROWS)
    return (rest // ROWS) * (NZ * ROWS) + wrapped(z + FIRST + k, NZ) * ROWS + rest % ROWS


def after(values, others):
    return lax.optimization_barrier((values, others))[0]


def gather_tokens(tokens, upstream, core, blocks):
    count = tokens.shape[0] // 2
    mine = jnp.stack(
        [lax.dynamic_slice_in_dim(v, core * count, count, axis=0) for v in (tokens, upstream)]
    )
    right = ring(mine, "y", 1, NY)
    left = ring(mine, "y", -1, NY)
    right, left = after((right, left), (blocks[2], blocks[NZ - 2]))
    half = count // 2
    far = jnp.concatenate(
        [ring(right[:, :half], "y", 1, NY), ring(left[:, half:], "y", -1, NY)], axis=1
    )
    groups = after(jnp.stack([left, far, right]), (blocks[3], blocks[NZ - 3]))
    other = ring(groups, "core", 1, NCORE)
    return tuple(
        jnp.concatenate([v] + [g[j, i] for g in (groups, other) for j in range(NY - 1)], axis=0)
        for i, v in enumerate((tokens, upstream))
    )


def scatter_grads(far, block, beside):
    half = NY // 2

    def plus(a, b):
        return (a.astype(f32) + b.astype(f32)).astype(bf16)

    right = ring(far[:half], "z", 1, NZ)
    left = ring(far[half:], "z", -1, NZ)
    up, down = block(NZ // 2 - 1), block(NZ // 2 + 1)
    up = jnp.concatenate([plus(up[:half], right), up[half:]], axis=0)
    down = jnp.concatenate([down[:half], plus(down[half:], left)], axis=0)
    for step in range(NZ // 2 - 2, 0, -1):
        up = plus(block(step), ring(up, "z", 1, NZ))
        down = plus(block(NZ - step), ring(down, "z", -1, NZ))
    up, down, beside = lax.optimization_barrier((up, down, beside))
    up, down = ring(up, "z", 1, NZ), ring(down, "z", -1, NZ)
    return (block(0).astype(f32) + up.astype(f32) + down.astype(f32)).astype(bf16), beside


def new_rows_of_grads(grads, new_start, p):
    block = along_dp(grads, 1)
    before = along_dp(grads[-EDGE:], 2)
    after = along_dp(grads[:EDGE], -1)
    window = jnp.concatenate([before, block, grads, after], axis=0)
    return rows_from(window, new_start - (ROWS * (p - 1) - EDGE), CAP_NEW, 0, 32)


def body(tokens, out_grad, master, moment_one, moment_two, old_offsets, new_offsets):
    y, z, core = lax.axis_index("y"), lax.axis_index("z"), lax.axis_index("core")
    p = y * NZ + z
    old_start = old_offsets[p]
    old_before = old_offsets[jnp.maximum(p - 1, 0)]
    new_start, new_end = new_offsets[p], new_offsets[p + 1]
    live = new_start != new_end
    scale_in = FEATURE_WIDTH ** (-0.5)
    scale_hidden = FF ** (-0.5)

    def dot(a, b, contract=(1, 0)):
        return lax.dot_general(
            a, b, (((contract[0],), (contract[1],)), ((), ())), preferred_element_type=f32
        )

    states = (master, moment_one, moment_two)
    split = split_rows(master, old_start - ROWS * p, old_offsets[p + 1] - old_start)
    first_left = along_dp(moment_one.astype(bf16), 1)
    split, first_left = lax.optimization_barrier((split, first_left))
    own = swap_along_y(split, y)

    order = jnp.arange(FEATURE_WIDTH, dtype=jnp.int32)[:, None] == ring_order(z)[None, :]
    order = order.astype(bf16)
    upstream = jnp.where(live, out_grad, jnp.zeros_like(out_grad))
    moved = [dot(v, order).astype(bf16) for v in (tokens, upstream)]
    moved = after(moved, own)
    blocks = gather_weights(own)
    tokens_all, upstream_all = gather_tokens(*moved, core, blocks)
    late = after(jnp.stack([master, moment_two]), (blocks[3], blocks[NZ - 3]))
    late_left = along_dp(late.astype(bf16), 1)

    chosen = [(FIRST + j) % NZ for j in range(NZ)]
    near_rows = joined(blocks, chosen[:NEAR], z)
    rest_rows = joined(blocks, chosen[NEAR:], z)
    split_at = NEAR * WIDTH

    def product(v, first, last):
        return dot(v[:, :split_at], near_rows[:, first:last]) + dot(
            v[:, split_at:], rest_rows[:, first:last]
        )

    gate_up = product(tokens_all, 0, 2 * WIDE) * scale_in
    gate, up = gate_up[:, :WIDE], gate_up[:, WIDE:]
    back = product(upstream_all, 2 * WIDE, 3 * WIDE) * scale_hidden
    sigmoid = jax.nn.sigmoid(gate)
    hidden = (gate * sigmoid * up).astype(bf16)
    gate_grad = (back * up * sigmoid * (1.0 + gate * (1.0 - sigmoid))).astype(bf16)
    up_grad = (back * gate * sigmoid).astype(bf16)
    both_grad = jnp.concatenate([gate_grad, up_grad], axis=1)
    both_grad, hidden, late_left = lax.optimization_barrier((both_grad, hidden, late_left))

    def terms(k):
        at = (k - FIRST) % NZ
        columns = slice(at * WIDTH, (at + 1) * WIDTH)
        top = dot(tokens_all[:, columns], both_grad, (0, 0)) * scale_in
        low = dot(upstream_all[:, columns], hidden, (0, 0)) * scale_hidden
        return jnp.concatenate([top.astype(bf16), low.astype(bf16)], axis=1).reshape(NY, ROWS, 3 * WIDE)

    far = terms(NZ // 2)
    hidden_in, far = lax.optimization_barrier((hidden, far))
    own_rows = tokens.shape[0]
    shared_rows = (hidden_in.shape[0] - own_rows) // NCORE
    mine, other = (hidden_in[own_rows + c * shared_rows :][:shared_rows] for c in range(NCORE))
    hidden_in = jnp.concatenate(
        [hidden_in[:own_rows], jnp.where(core == 0, mine, other), jnp.where(core == 0, other, mine)],
        axis=0,
    )
    in_ring = jnp.concatenate([near_rows, rest_rows], axis=0)[:, 2 * WIDE :]
    in_ring = in_ring.reshape(NZ, NY, ROWS, WIDE)
    in_ring = jnp.concatenate([in_ring, in_ring], axis=0)
    down_weight = lax.dynamic_slice_in_dim(in_ring, NZ - wrapped(z + FIRST, NZ), NZ, axis=0)
    down_weight = jnp.transpose(down_weight, (1, 0, 2, 3)).reshape(FEATURE_WIDTH, WIDE)
    partial = (dot(hidden_in, down_weight, (1, 1)) * scale_hidden).astype(bf16)
    shared = lax.psum_scatter(partial, MP, scatter_dimension=1, tiled=True)
    shares = shared[own_rows:].reshape(NCORE, NY - 1, own_rows // NCORE, -1)
    total = shared[:own_rows].astype(f32)
    for step in range(1, NY):
        share = shares[:, step - 1].reshape(own_rows, -1)
        total = total + ring(share, "y", step, NY).astype(f32)
    layer_output = jnp.where(live, total, 0.0).astype(bf16)

    slots = jnp.arange(CAP_NEW, dtype=jnp.int32)
    row = new_start + slots
    held = []
    for own_state, left in zip(states, (late_left[0], first_left, late_left[1])):
        moved = rows_from(left, new_start - old_before, CAP_NEW, 0, CAP_NEW).astype(f32)
        kept = rows_from(own_state, new_start - old_start, CAP_NEW, 72, 16)
        held.append(jnp.where(row_mask(row < old_start), moved, kept))

    summed, (held, layer_output) = scatter_grads(far, terms, (held, layer_output))
    quarters = swap_along_y(summed, y)
    quarters = quarters.reshape(NY, ROWS, 3, WIDE)[..., :QUART]
    grads = jnp.transpose(quarters, (1, 2, 0, 3)).reshape(ROWS, 3, COLS)
    grads = new_rows_of_grads(grads, new_start, p).astype(f32)
    updated = adam_step(*held, grads)
    in_range = row_mask(row < new_end)
    return tuple(jnp.where(in_range, v, 0.0) for v in updated) + (layer_output,)


def solution(mesh):
    grid = Mesh(mesh.devices.reshape(NY, NZ, NX, NCORE), DP + MP)
    state = P(DP, None, MP)
    return jax.shard_map(
        body,
        mesh=grid,
        in_specs=(P(DP, None), P(DP, None), state, state, state, P(), P()),
        out_specs=(state, state, state, P(DP, MP)),
        check_vma=False,
    )
```

```python
import jax
import jax.numpy as jnp
from jax import lax
from jax.sharding import Mesh, PartitionSpec as P

FEATURE_WIDTH = 2048
FF = 7168
NY, NZ, NX, NCORE = 4, 8, 4, 2
ROWS = 64
CAP_OLD = 70
CAP_NEW = 86
COLS = 896
QUART = COLS // NY
WIDE = 256
EDGE = 4
SENT = ROWS + 2 * EDGE

beta_one = 0.9
beta_two = 0.95
learn_rate = 0.01
decay_rate = 0.1
adam_eps = 1e-08
bias_one = 1.0 - 0.9**10
bias_two = 1.0 - 0.95**10

bf16 = jnp.bfloat16
f32 = jnp.float32
DP = ("y", "z")
MP = ("x", "core")


def ring(value, axis, by, size):
    return lax.ppermute(value, axis, [(i, (i + by) % size) for i in range(size)])


def wrapped(index, size):
    return lax.rem(index + size, jnp.int32(size))


def along_dp(value, by):
    peers = NY * NZ
    pairs = [(i, i + by) for i in range(peers) if 0 <= i + by < peers]
    return lax.ppermute(value, DP, pairs)


def rows_from(value, start, count, front, back):
    padding = [(front, back)] + [(0, 0)] * (value.ndim - 1)
    return lax.dynamic_slice_in_dim(jnp.pad(value, padding), front + start, count, axis=0)


def row_mask(condition):
    return condition[:, None, None]


def adam_step(master_rows, first_rows, second_rows, grads):
    first_new = beta_one * first_rows + (1.0 - beta_one) * grads
    second_new = beta_two * second_rows + (1.0 - beta_two) * grads * grads
    update = first_new / bias_one / (jnp.sqrt(second_new / bias_two) + adam_eps)
    master_new = master_rows - learn_rate * (update + decay_rate * master_rows)
    return (master_new, first_new, second_new)


def swap_along_y(pieces, y):
    def piece(step):
        return lax.dynamic_slice_in_dim(pieces, wrapped(y + step, NY), 1, axis=0)

    order = [piece(0)] + [ring(piece(step), "y", step, NY) for step in range(1, NY)]
    order = [order[0]] + order[:0:-1]
    return jnp.concatenate(
        [lax.select_n(wrapped(i - y, NY), *order) for i in range(NY)], axis=0
    )


def split_rows(master, shift, held):
    slots = jnp.arange(CAP_OLD, dtype=jnp.int32)
    own = jnp.where(row_mask(slots < held), master, 0.0).astype(bf16)
    rows = jnp.concatenate(
        [
            rows_from(own, -shift, ROWS, 16, 16),
            rows_from(own, -shift - EDGE, EDGE, 16, 16),
            rows_from(own, ROWS - shift, EDGE, 16, 16),
        ],
        axis=0,
    )
    split = rows.reshape(SENT, 3, NY, QUART)
    split = jnp.pad(split, ((0, 0), (0, 0), (0, 0), (0, WIDE - QUART)))
    return jnp.transpose(split, (2, 0, 1, 3)).reshape(NY, SENT, 3 * WIDE)


def gather_weights(own):
    blocks = {0: own}
    right, left = own, own
    for step in range(1, NZ // 2):
        right = ring(right, "z", 1, NZ)
        left = ring(left, "z", -1, NZ)
        blocks[-step] = right
        blocks[step] = left
    half = NY // 2
    far_low = ring(right[:half], "z", 1, NZ)
    far_high = ring(left[half:], "z", -1, NZ)
    blocks[NZ // 2] = jnp.concatenate([far_low, far_high], axis=0)
    return blocks


def joined(blocks, z):
    full = jnp.zeros((NY, NZ, SENT, 3 * WIDE), bf16)
    for step, block in blocks.items():
        full = lax.dynamic_update_slice_in_dim(full, block[:, None], wrapped(z + step, NZ), axis=1)
    full = full.reshape(NY * NZ, SENT, 3 * WIDE)
    none = jnp.zeros((1, EDGE, 3 * WIDE), bf16)
    before = jnp.concatenate([full[1:, ROWS : ROWS + EDGE], none], axis=0)
    behind = jnp.concatenate([none, full[:-1, ROWS + EDGE :]], axis=0)
    main = full[:, :ROWS]
    main = jnp.concatenate(
        [main[:, :EDGE] + behind, main[:, EDGE:-EDGE], main[:, -EDGE:] + before], axis=1
    )
    return main.reshape(FEATURE_WIDTH, 3 * WIDE)


def after(values, others):
    return lax.optimization_barrier((values, others))[0]


def gather_tokens(tokens, upstream, core, blocks):
    count = tokens.shape[0] // 2
    mine = jnp.stack(
        [lax.dynamic_slice_in_dim(v, core * count, count, axis=0) for v in (tokens, upstream)]
    )
    right = ring(mine, "y", 1, NY)
    left = ring(mine, "y", -1, NY)
    right, left = after((right, left), (blocks[2], blocks[-2]))
    half = count // 2
    far = jnp.concatenate(
        [ring(right[:, :half], "y", 1, NY), ring(left[:, half:], "y", -1, NY)], axis=1
    )
    groups = after(jnp.stack([left, far, right]), (blocks[3], blocks[-3]))
    other = ring(groups, "core", 1, NCORE)
    first = jnp.where(core == 0, groups, other)
    second = jnp.where(core == 0, other, groups)
    both = jnp.concatenate([first, second], axis=2)
    return tuple(
        jnp.concatenate([v, both[0, i], both[1, i], both[2, i]], axis=0)
        for i, v in enumerate((tokens, upstream))
    )


def scatter_grads(terms, z, beside):
    terms = terms.reshape(NY, NZ, ROWS, 3 * WIDE)

    def block(step):
        return lax.dynamic_slice_in_dim(terms, wrapped(z + step, NZ), 1, axis=1)[:, 0]

    half = NY // 2

    def plus(a, b):
        return (a.astype(f32) + b.astype(f32)).astype(bf16)

    far = block(NZ // 2)
    right = ring(far[:half], "z", 1, NZ)
    left = ring(far[half:], "z", -1, NZ)
    up, down = block(NZ // 2 - 1), block(1 - NZ // 2)
    up = jnp.concatenate([plus(up[:half], right), up[half:]], axis=0)
    down = jnp.concatenate([down[:half], plus(down[half:], left)], axis=0)
    for step in range(NZ // 2 - 2, 0, -1):
        up = plus(block(step), ring(up, "z", 1, NZ))
        down = plus(block(-step), ring(down, "z", -1, NZ))
    up, down, beside = lax.optimization_barrier((up, down, beside))
    up, down = ring(up, "z", 1, NZ), ring(down, "z", -1, NZ)
    return (block(0).astype(f32) + up.astype(f32) + down.astype(f32)).astype(bf16), beside


def new_rows_of_grads(grads, new_start, p):
    block = along_dp(grads, 1)
    before = along_dp(grads[-EDGE:], 2)
    after = along_dp(grads[:EDGE], -1)
    window = jnp.concatenate([before, block, grads, after], axis=0)
    return rows_from(window, new_start - (ROWS * (p - 1) - EDGE), CAP_NEW, 0, 32)


def body(tokens, out_grad, master, moment_one, moment_two, old_offsets, new_offsets):
    y, z, core = lax.axis_index("y"), lax.axis_index("z"), lax.axis_index("core")
    p = y * NZ + z
    old_start = old_offsets[p]
    old_before = old_offsets[jnp.maximum(p - 1, 0)]
    new_start, new_end = new_offsets[p], new_offsets[p + 1]
    live = new_start != new_end
    scale_in = FEATURE_WIDTH ** (-0.5)
    scale_hidden = FF ** (-0.5)

    upstream = jnp.where(live, out_grad, jnp.zeros_like(out_grad))
    split = split_rows(master, old_start - ROWS * p, old_offsets[p + 1] - old_start)
    first_left = moment_one.astype(bf16)
    split, first_left = lax.optimization_barrier((split, first_left))
    own = swap_along_y(split, y)
    first_left = ring(first_left, "z", 1, NZ)
    own, first_left = lax.optimization_barrier((own, first_left))
    tokens_in, upstream = after((tokens, upstream), own)
    blocks = gather_weights(own)
    tokens_all, upstream_all = gather_tokens(tokens_in, upstream, core, blocks)
    states = (master, moment_one, moment_two)
    blocks[NZ // 2], late, first_left = lax.optimization_barrier(
        (blocks[NZ // 2], master, first_left)
    )
    master_left = along_dp(late.astype(bf16), 1)
    turns = [(i * NZ, (i + 1) * NZ) for i in range(NY - 1)]
    first_left = jnp.where(z == 0, lax.ppermute(first_left, DP, turns), first_left)
    weights = joined(blocks, z)

    def dot(a, b, contract=(1, 0)):
        return lax.dot_general(
            a, b, (((contract[0],), (contract[1],)), ((), ())), preferred_element_type=f32
        )

    gate_up = dot(tokens_all, weights[:, : 2 * WIDE]) * scale_in
    gate, up = gate_up[:, :WIDE], gate_up[:, WIDE:]
    down_weight = weights[:, 2 * WIDE :]
    back = dot(upstream_all, down_weight) * scale_hidden
    sigmoid = jax.nn.sigmoid(gate)
    hidden = (gate * sigmoid * up).astype(bf16)
    gate_grad = (back * up * sigmoid * (1.0 + gate * (1.0 - sigmoid))).astype(bf16)
    up_grad = (back * gate * sigmoid).astype(bf16)
    partial = (dot(hidden, down_weight, (1, 1)) * scale_hidden).astype(bf16)
    terms = jnp.concatenate(
        [
            (dot(tokens_all, jnp.concatenate([gate_grad, up_grad], axis=1), (0, 0)) * scale_in).astype(bf16),
            (dot(upstream_all, hidden, (0, 0)) * scale_hidden).astype(bf16),
        ],
        axis=1,
    )

    shared = lax.psum_scatter(partial, MP, scatter_dimension=1, tiled=True)
    shared = shared.reshape(NY, tokens.shape[0], -1)
    total = shared[0].astype(f32)
    for step in range(1, NY):
        total = total + ring(shared[step], "y", step, NY).astype(f32)
    layer_output = jnp.where(live, total, 0.0).astype(bf16)

    terms, master_left, late = lax.optimization_barrier((terms, master_left, moment_two))
    from_left = (master_left, first_left, along_dp(late.astype(bf16), 1))
    slots = jnp.arange(CAP_NEW, dtype=jnp.int32)
    row = new_start + slots
    held = []
    for own_state, left in zip(states, from_left):
        moved = rows_from(left, new_start - old_before, CAP_NEW, 0, CAP_NEW).astype(f32)
        kept = rows_from(own_state, new_start - old_start, CAP_NEW, 72, 16)
        held.append(jnp.where(row_mask(row < old_start), moved, kept))

    summed, (held, layer_output) = scatter_grads(terms, z, (held, layer_output))
    quarters = swap_along_y(summed, y)
    quarters = quarters.reshape(NY, ROWS, 3, WIDE)[..., :QUART]
    grads = jnp.transpose(quarters, (1, 2, 0, 3)).reshape(ROWS, 3, COLS)
    grads = new_rows_of_grads(grads, new_start, p).astype(f32)

    updated = adam_step(*held, grads)
    in_range = row_mask(row < new_end)
    return tuple(jnp.where(in_range, v, 0.0) for v in updated) + (layer_output,)


def solution(mesh):
    grid = Mesh(mesh.devices.reshape(NY, NZ, NX, NCORE), DP + MP)
    state = P(DP, None, MP)
    return jax.shard_map(
        body,
        mesh=grid,
        in_specs=(P(DP, None), P(DP, None), state, state, state, P(), P()),
        out_specs=(state, state, state, P(DP, MP)),
        check_vma=False,
    )
```

```python
import jax
import jax.numpy as jnp
from jax import lax
from jax.sharding import Mesh, PartitionSpec as P

FEATURE_WIDTH = 2048
FF = 7168
NY, NZ, NX, NCORE = 4, 8, 4, 2
ROWS = 64
TOK_DEV = 256
CAP_OLD = 70
CAP_NEW = 86
COLS = 896
QUART = COLS // NY
WIDE = 256
EDGE = 4
SENT = ROWS + 2 * EDGE

beta_one = 0.9
beta_two = 0.95
learn_rate = 0.01
decay_rate = 0.1
adam_eps = 1e-08
bias_one = 1.0 - 0.9**10
bias_two = 1.0 - 0.95**10

bf16 = jnp.bfloat16
f32 = jnp.float32
DP = ("y", "z")
MP = ("x", "core")


def ring(value, axis, by, size):
    return lax.ppermute(value, axis, [(i, (i + by) % size) for i in range(size)])


def wrapped(index, size):
    return lax.rem(index + size, jnp.int32(size))


def along_dp(value, by):
    peers = NY * NZ
    pairs = [(i, i + by) for i in range(peers) if 0 <= i + by < peers]
    return lax.ppermute(value, DP, pairs)


def rows_from(value, start, count, front, back):
    padding = [(front, back)] + [(0, 0)] * (value.ndim - 1)
    return lax.dynamic_slice_in_dim(jnp.pad(value, padding), front + start, count, axis=0)


def row_mask(condition):
    return condition[:, None, None]


def adam_step(master_rows, first_rows, second_rows, grads):
    first_new = beta_one * first_rows + (1.0 - beta_one) * grads
    second_new = beta_two * second_rows + (1.0 - beta_two) * grads * grads
    update = first_new / bias_one / (jnp.sqrt(second_new / bias_two) + adam_eps)
    master_new = master_rows - learn_rate * (update + decay_rate * master_rows)
    return (master_new, first_new, second_new)


def swap_along_y(pieces, y):
    def piece(step):
        return lax.dynamic_slice_in_dim(pieces, wrapped(y + step, NY), 1, axis=0)

    order = [piece(0)] + [ring(piece(step), "y", step, NY) for step in range(1, NY)]
    order = [order[0]] + order[:0:-1]
    return jnp.concatenate(
        [lax.select_n(wrapped(i - y, NY), *order) for i in range(NY)], axis=0
    )


def split_rows(master, shift, held):
    slots = jnp.arange(CAP_OLD, dtype=jnp.int32)
    own = jnp.where(row_mask(slots < held), master, 0.0).astype(bf16)
    rows = jnp.concatenate(
        [
            rows_from(own, -shift, ROWS, 16, 16),
            rows_from(own, -shift - EDGE, EDGE, 16, 16),
            rows_from(own, ROWS - shift, EDGE, 16, 16),
        ],
        axis=0,
    )
    split = rows.reshape(SENT, 3, NY, QUART)
    split = jnp.pad(split, ((0, 0), (0, 0), (0, 0), (0, WIDE - QUART)))
    return jnp.transpose(split, (2, 0, 1, 3)).reshape(NY, SENT, 3 * WIDE)


def gather_weights(own, beside):
    blocks = {0: own}
    right, left = own, own
    for step in range(1, NZ // 2):
        right = ring(right, "z", 1, NZ)
        left = ring(left, "z", -1, NZ)
        if step == 1:
            right, left, beside = lax.optimization_barrier((right, left, beside))
        blocks[-step] = right
        blocks[step] = left
    half = NY // 2
    far_low = ring(right[:half], "z", 1, NZ)
    far_high = ring(left[half:], "z", -1, NZ)
    blocks[NZ // 2] = jnp.concatenate([far_low, far_high], axis=0)
    return blocks, beside


def joined(blocks, z):
    full = jnp.zeros((NY, NZ, SENT, 3 * WIDE), bf16)
    for step, block in blocks.items():
        full = lax.dynamic_update_slice_in_dim(full, block[:, None], wrapped(z + step, NZ), axis=1)
    full = full.reshape(NY * NZ, SENT, 3 * WIDE)
    none = jnp.zeros((1, EDGE, 3 * WIDE), bf16)
    before = jnp.concatenate([full[1:, ROWS : ROWS + EDGE], none], axis=0)
    behind = jnp.concatenate([none, full[:-1, ROWS + EDGE :]], axis=0)
    behind = jnp.pad(behind, ((0, 0), (0, ROWS - EDGE), (0, 0)))
    before = jnp.pad(before, ((0, 0), (ROWS - EDGE, 0), (0, 0)))
    return (full[:, :ROWS] + behind + before).reshape(FEATURE_WIDTH, 3 * WIDE)


def after(values, others):
    return lax.optimization_barrier((values, others))[0]


def gather_tokens(tokens, upstream, core, blocks):
    count = tokens.shape[0] // 2
    mine = jnp.stack(
        [lax.dynamic_slice_in_dim(v, core * count, count, axis=0) for v in (tokens, upstream)]
    )
    right = ring(mine, "y", 1, NY)
    left = ring(mine, "y", -1, NY)
    right, left = after((right, left), (blocks[2], blocks[-2]))
    half = count // 2
    far = jnp.concatenate(
        [ring(right[:, :half], "y", 1, NY), ring(left[:, half:], "y", -1, NY)], axis=1
    )
    groups = after(jnp.stack([left, far, right]), (blocks[3], blocks[-3]))
    other = ring(groups, "core", 1, NCORE)
    return tuple(
        jnp.concatenate([v] + [g[j, i] for g in (groups, other) for j in range(NY - 1)], axis=0)
        for i, v in enumerate((tokens, upstream))
    )


def in_order(rows, y, core):
    half = TOK_DEV // NCORE

    def part(at):
        return rows[TOK_DEV + at * half :][:half]

    groups = [rows[:TOK_DEV]]
    for j in range(NY - 1):
        mine, other = part(j), part(NY - 1 + j)
        pair = [jnp.where(core == 0, mine, other), jnp.where(core == 0, other, mine)]
        groups.append(jnp.concatenate(pair, axis=0))
    return jnp.concatenate(
        [lax.select_n(wrapped(i - y, NY), *groups) for i in range(NY)], axis=0
    )


def scatter_grads(terms, z, beside):
    terms = terms.reshape(NY, NZ, ROWS, 3 * WIDE)

    def block(step):
        return lax.dynamic_slice_in_dim(terms, wrapped(z + step, NZ), 1, axis=1)[:, 0]

    half = NY // 2

    def plus(a, b):
        return (a.astype(f32) + b.astype(f32)).astype(bf16)

    far = block(NZ // 2)
    right = ring(far[:half], "z", 1, NZ)
    left = ring(far[half:], "z", -1, NZ)
    up, down = block(NZ // 2 - 1), block(1 - NZ // 2)
    up = jnp.concatenate([plus(up[:half], right), up[half:]], axis=0)
    down = jnp.concatenate([down[:half], plus(down[half:], left)], axis=0)
    for step in range(NZ // 2 - 2, 0, -1):
        up = plus(block(step), ring(up, "z", 1, NZ))
        down = plus(block(-step), ring(down, "z", -1, NZ))
    up, down, beside = lax.optimization_barrier((up, down, beside))
    up, down = ring(up, "z", 1, NZ), ring(down, "z", -1, NZ)
    return (block(0).astype(f32) + up.astype(f32) + down.astype(f32)).astype(bf16), beside


def new_rows_of_grads(grads, new_start, p):
    block = along_dp(grads, 1)
    before = along_dp(grads[-EDGE:], 2)
    after = along_dp(grads[:EDGE], -1)
    window = jnp.concatenate([before, block, grads, after], axis=0)
    return rows_from(window, new_start - (ROWS * (p - 1) - EDGE), CAP_NEW, 0, 32)


def body(tokens, out_grad, master, moment_one, moment_two, old_offsets, new_offsets):
    y, z, core = lax.axis_index("y"), lax.axis_index("z"), lax.axis_index("core")
    p = y * NZ + z
    old_start = old_offsets[p]
    old_before = old_offsets[jnp.maximum(p - 1, 0)]
    new_start, new_end = new_offsets[p], new_offsets[p + 1]
    live = new_start != new_end
    scale_in = FEATURE_WIDTH ** (-0.5)
    scale_hidden = FF ** (-0.5)

    upstream = jnp.where(live, out_grad, jnp.zeros_like(out_grad))
    split = split_rows(master, old_start - ROWS * p, old_offsets[p + 1] - old_start)
    states = (master, moment_one, moment_two)
    from_left = ring(jnp.stack([v.astype(bf16) for v in states]), "z", 1, NZ)
    own = swap_along_y(split, y)
    tokens_in, upstream = after((tokens, upstream), own)
    blocks, from_left = gather_weights(own, from_left)
    tokens_all, upstream_all = gather_tokens(tokens_in, upstream, core, blocks)
    blocks[NZ // 2], from_left = lax.optimization_barrier((blocks[NZ // 2], from_left))
    turns = [(i * NZ, (i + 1) * NZ) for i in range(NY - 1)]
    from_left = jnp.where(z == 0, lax.ppermute(from_left, DP, turns), from_left)
    weights = joined(blocks, z)

    def dot(a, b, contract=(1, 0)):
        return lax.dot_general(
            a, b, (((contract[0],), (contract[1],)), ((), ())), preferred_element_type=f32
        )

    gate_up = dot(tokens_all, weights[:, : 2 * WIDE]) * scale_in
    gate, up = gate_up[:, :WIDE], gate_up[:, WIDE:]
    down_weight = weights[:, 2 * WIDE :]
    back = dot(upstream_all, down_weight) * scale_hidden
    sigmoid = jax.nn.sigmoid(gate)
    hidden = (gate * sigmoid * up).astype(bf16)
    gate_grad = (back * up * sigmoid * (1.0 + gate * (1.0 - sigmoid))).astype(bf16)
    up_grad = (back * gate * sigmoid).astype(bf16)
    partial = (dot(in_order(hidden, y, core), down_weight, (1, 1)) * scale_hidden).astype(bf16)
    terms = jnp.concatenate(
        [
            (dot(tokens_all, jnp.concatenate([gate_grad, up_grad], axis=1), (0, 0)) * scale_in).astype(bf16),
            (dot(upstream_all, hidden, (0, 0)) * scale_hidden).astype(bf16),
        ],
        axis=1,
    )

    shared = lax.psum_scatter(partial, MP, scatter_dimension=1, tiled=True)
    slots = jnp.arange(CAP_NEW, dtype=jnp.int32)
    row = new_start + slots
    held = []
    for own_state, left in zip(states, from_left):
        moved = rows_from(left, new_start - old_before, CAP_NEW, 0, CAP_NEW).astype(f32)
        kept = rows_from(own_state, new_start - old_start, CAP_NEW, 72, 16)
        held.append(jnp.where(row_mask(row < old_start), moved, kept))

    summed, (held, shared) = scatter_grads(terms, z, (held, shared))
    total = lax.psum_scatter(shared, "y", scatter_dimension=0, tiled=True)
    layer_output = jnp.where(live, total, jnp.zeros_like(total))
    quarters = swap_along_y(summed, y)
    quarters = quarters.reshape(NY, ROWS, 3, WIDE)[..., :QUART]
    grads = jnp.transpose(quarters, (1, 2, 0, 3)).reshape(ROWS, 3, COLS)
    grads = new_rows_of_grads(grads, new_start, p).astype(f32)

    updated = adam_step(*held, grads)
    in_range = row_mask(row < new_end)
    return tuple(jnp.where(in_range, v, 0.0) for v in updated) + (layer_output,)


def solution(mesh):
    grid = Mesh(mesh.devices.reshape(NY, NZ, NX, NCORE), DP + MP)
    state = P(DP, None, MP)
    return jax.shard_map(
        body,
        mesh=grid,
        in_specs=(P(DP, None), P(DP, None), state, state, state, P(), P()),
        out_specs=(state, state, state, P(DP, MP)),
        check_vma=False,
    )
```

```python
import jax
import jax.numpy as jnp
from jax import lax
from jax.sharding import Mesh, PartitionSpec as P

FEATURE_WIDTH = 2048
FF = 7168
NY, NZ, NX, NCORE = 4, 8, 4, 2
ROWS = 64
TOK_DEV = 256
CAP_OLD = 70
CAP_NEW = 86
COLS = 896
QUART = COLS // NY
WIDE = 256
EDGE = 4
SENT = ROWS + 2 * EDGE

beta_one = 0.9
beta_two = 0.95
learn_rate = 0.01
decay_rate = 0.1
adam_eps = 1e-08
bias_one = 1.0 - 0.9**10
bias_two = 1.0 - 0.95**10

bf16 = jnp.bfloat16
f32 = jnp.float32
DP = ("y", "z")
MP = ("x", "core")


def ring(value, axis, by, size):
    return lax.ppermute(value, axis, [(i, (i + by) % size) for i in range(size)])


def wrapped(index, size):
    return lax.rem(index + size, jnp.int32(size))


def along_dp(value, by):
    peers = NY * NZ
    pairs = [(i, i + by) for i in range(peers) if 0 <= i + by < peers]
    return lax.ppermute(value, DP, pairs)


def rows_from(value, start, count, front, back):
    padding = [(front, back)] + [(0, 0)] * (value.ndim - 1)
    return lax.dynamic_slice_in_dim(jnp.pad(value, padding), front + start, count, axis=0)


def row_mask(condition):
    return condition[:, None, None]


def adam_step(master_rows, first_rows, second_rows, grads):
    first_new = beta_one * first_rows + (1.0 - beta_one) * grads
    second_new = beta_two * second_rows + (1.0 - beta_two) * grads * grads
    update = first_new / bias_one / (jnp.sqrt(second_new / bias_two) + adam_eps)
    master_new = master_rows - learn_rate * (update + decay_rate * master_rows)
    return (master_new, first_new, second_new)


def swap_along_y(pieces, y):
    def piece(step):
        return lax.dynamic_slice_in_dim(pieces, wrapped(y + step, NY), 1, axis=0)

    order = [piece(0)] + [ring(piece(step), "y", step, NY) for step in range(1, NY)]
    order = [order[0]] + order[:0:-1]
    return jnp.concatenate(
        [lax.select_n(wrapped(i - y, NY), *order) for i in range(NY)], axis=0
    )


def split_rows(master, shift, held):
    slots = jnp.arange(CAP_OLD, dtype=jnp.int32)
    own = jnp.where(row_mask(slots < held), master, 0.0).astype(bf16)
    rows = jnp.concatenate(
        [
            rows_from(own, -shift, ROWS, 16, 16),
            rows_from(own, -shift - EDGE, EDGE, 16, 16),
            rows_from(own, ROWS - shift, EDGE, 16, 16),
        ],
        axis=0,
    )
    split = rows.reshape(SENT, 3, NY, QUART)
    split = jnp.pad(split, ((0, 0), (0, 0), (0, 0), (0, WIDE - QUART)))
    return jnp.transpose(split, (2, 0, 1, 3)).reshape(NY, SENT, 3 * WIDE)


def gather_weights(own):
    blocks = {0: own}
    right, left = own, own
    for step in range(1, NZ // 2):
        right = ring(right, "z", 1, NZ)
        left = ring(left, "z", -1, NZ)
        blocks[-step] = right
        blocks[step] = left
    half = NY // 2
    far_low = ring(right[:half], "z", 1, NZ)
    far_high = ring(left[half:], "z", -1, NZ)
    blocks[NZ // 2] = jnp.concatenate([far_low, far_high], axis=0)
    return blocks


def joined(blocks, z):
    full = jnp.zeros((NY, NZ, SENT, 3 * WIDE), bf16)
    for step, block in blocks.items():
        full = lax.dynamic_update_slice_in_dim(full, block[:, None], wrapped(z + step, NZ), axis=1)
    full = full.reshape(NY * NZ, SENT, 3 * WIDE)
    none = jnp.zeros((1, EDGE, 3 * WIDE), bf16)
    before = jnp.concatenate([full[1:, ROWS : ROWS + EDGE], none], axis=0)
    behind = jnp.concatenate([none, full[:-1, ROWS + EDGE :]], axis=0)
    behind = jnp.pad(behind, ((0, 0), (0, ROWS - EDGE), (0, 0)))
    before = jnp.pad(before, ((0, 0), (ROWS - EDGE, 0), (0, 0)))
    return (full[:, :ROWS] + behind + before).reshape(FEATURE_WIDTH, 3 * WIDE)


def after(values, others):
    return lax.optimization_barrier((values, others))[0]


def gather_tokens(tokens, upstream, core, blocks):
    count = tokens.shape[0] // 2
    mine = jnp.stack(
        [lax.dynamic_slice_in_dim(v, core * count, count, axis=0) for v in (tokens, upstream)]
    )
    right = ring(mine, "y", 1, NY)
    left = ring(mine, "y", -1, NY)
    right, left = after((right, left), (blocks[2], blocks[-2]))
    half = count // 2
    far = jnp.concatenate(
        [ring(right[:, :half], "y", 1, NY), ring(left[:, half:], "y", -1, NY)], axis=1
    )
    groups = after(jnp.stack([left, far, right]), (blocks[3], blocks[-3]))
    other = ring(groups, "core", 1, NCORE)
    return tuple(
        jnp.concatenate([v] + [g[j, i] for g in (groups, other) for j in range(NY - 1)], axis=0)
        for i, v in enumerate((tokens, upstream))
    )


def in_order(rows, y, core):
    half = TOK_DEV // NCORE

    def part(at):
        return rows[TOK_DEV + at * half :][:half]

    groups = [rows[:TOK_DEV]]
    for j in range(NY - 1):
        mine, other = part(j), part(NY - 1 + j)
        pair = [jnp.where(core == 0, mine, other), jnp.where(core == 0, other, mine)]
        groups.append(jnp.concatenate(pair, axis=0))
    return jnp.concatenate(
        [lax.select_n(wrapped(i - y, NY), *groups) for i in range(NY)], axis=0
    )


def scatter_grads(terms, z, beside):
    terms = [v.reshape(NY, NZ, ROWS, -1) for v in terms]

    def block(step):
        at = wrapped(z + step, NZ)
        return jnp.concatenate(
            [lax.dynamic_slice_in_dim(v, at, 1, axis=1)[:, 0] for v in terms], axis=2
        )

    half = NY // 2

    def plus(a, b):
        return (a.astype(f32) + b.astype(f32)).astype(bf16)

    far = block(NZ // 2)
    right = ring(far[:half], "z", 1, NZ)
    left = ring(far[half:], "z", -1, NZ)
    up, down = block(NZ // 2 - 1), block(1 - NZ // 2)
    up = jnp.concatenate([plus(up[:half], right), up[half:]], axis=0)
    down = jnp.concatenate([down[:half], plus(down[half:], left)], axis=0)
    for step in range(NZ // 2 - 2, 0, -1):
        up = plus(block(step), ring(up, "z", 1, NZ))
        down = plus(block(-step), ring(down, "z", -1, NZ))
    up, down, beside = lax.optimization_barrier((up, down, beside))
    up, down = ring(up, "z", 1, NZ), ring(down, "z", -1, NZ)
    return (block(0).astype(f32) + up.astype(f32) + down.astype(f32)).astype(bf16), beside


def new_rows_of_grads(grads, new_start, p):
    block = along_dp(grads, 1)
    before = along_dp(grads[-EDGE:], 2)
    after = along_dp(grads[:EDGE], -1)
    window = jnp.concatenate([before, block, grads, after], axis=0)
    return rows_from(window, new_start - (ROWS * (p - 1) - EDGE), CAP_NEW, 0, 32)


def body(tokens, out_grad, master, moment_one, moment_two, old_offsets, new_offsets):
    y, z, core = lax.axis_index("y"), lax.axis_index("z"), lax.axis_index("core")
    p = y * NZ + z
    old_start = old_offsets[p]
    old_before = old_offsets[jnp.maximum(p - 1, 0)]
    new_start, new_end = new_offsets[p], new_offsets[p + 1]
    live = new_start != new_end
    scale_in = FEATURE_WIDTH ** (-0.5)
    scale_hidden = FF ** (-0.5)

    upstream = jnp.where(live, out_grad, jnp.zeros_like(out_grad))
    split = split_rows(master, old_start - ROWS * p, old_offsets[p + 1] - old_start)
    states = (master, moment_one, moment_two)
    own = swap_along_y(split, y)
    tokens_in, upstream = after((tokens, upstream), own)
    blocks = gather_weights(own)
    tokens_all, upstream_all = gather_tokens(tokens_in, upstream, core, blocks)
    late = moment_two
    for k in (3, -3):
        blocks[k], late = lax.optimization_barrier((blocks[k], late))
    blocks[NZ // 2], later = lax.optimization_barrier((blocks[NZ // 2], master))
    second_left = along_dp(late.astype(bf16), 1)
    master_left = along_dp(later.astype(bf16), 1)
    weights = joined(blocks, z)

    def dot(a, b, contract=(1, 0)):
        return lax.dot_general(
            a, b, (((contract[0],), (contract[1],)), ((), ())), preferred_element_type=f32
        )

    gate_up = dot(tokens_all, weights[:, : 2 * WIDE]) * scale_in
    gate, up = gate_up[:, :WIDE], gate_up[:, WIDE:]
    down_weight = weights[:, 2 * WIDE :]
    back = dot(upstream_all, down_weight) * scale_hidden
    sigmoid = jax.nn.sigmoid(gate)
    hidden = (gate * sigmoid * up).astype(bf16)
    gate_grad = (back * up * sigmoid * (1.0 + gate * (1.0 - sigmoid))).astype(bf16)
    up_grad = (back * gate * sigmoid).astype(bf16)
    hidden, gate_grad, up_grad, second_left = lax.optimization_barrier(
        (hidden, gate_grad, up_grad, second_left)
    )
    partial = (dot(in_order(hidden, y, core), down_weight, (1, 1)) * scale_hidden).astype(bf16)
    both_grad = jnp.concatenate([gate_grad, up_grad], axis=1)
    top = (dot(tokens_all, both_grad, (0, 0)) * scale_in).astype(bf16)
    low = (dot(upstream_all, hidden, (0, 0)) * scale_hidden).astype(bf16)
    top, low, master_left, latest = lax.optimization_barrier((top, low, master_left, moment_one))
    first_left = along_dp(latest.astype(bf16), 1)
    from_left = (master_left, first_left, second_left)

    shared = lax.psum_scatter(partial, MP, scatter_dimension=1, tiled=True)
    slots = jnp.arange(CAP_NEW, dtype=jnp.int32)
    row = new_start + slots
    held = []
    for own_state, left in zip(states, from_left):
        moved = rows_from(left, new_start - old_before, CAP_NEW, 0, CAP_NEW).astype(f32)
        kept = rows_from(own_state, new_start - old_start, CAP_NEW, 72, 16)
        held.append(jnp.where(row_mask(row < old_start), moved, kept))

    summed, (held, shared) = scatter_grads((top, low), z, (held, shared))
    total = lax.psum_scatter(shared, "y", scatter_dimension=0, tiled=True)
    layer_output = jnp.where(live, total, jnp.zeros_like(total))
    quarters = swap_along_y(summed, y)
    quarters = quarters.reshape(NY, ROWS, 3, WIDE)[..., :QUART]
    grads = jnp.transpose(quarters, (1, 2, 0, 3)).reshape(ROWS, 3, COLS)
    grads = new_rows_of_grads(grads, new_start, p).astype(f32)

    updated = adam_step(*held, grads)
    in_range = row_mask(row < new_end)
    return tuple(jnp.where(in_range, v, 0.0) for v in updated) + (layer_output,)


def solution(mesh):
    grid = Mesh(mesh.devices.reshape(NY, NZ, NX, NCORE), DP + MP)
    state = P(DP, None, MP)
    return jax.shard_map(
        body,
        mesh=grid,
        in_specs=(P(DP, None), P(DP, None), state, state, state, P(), P()),
        out_specs=(state, state, state, P(DP, MP)),
        check_vma=False,
    )
```

```python
import jax
import jax.numpy as jnp
from jax import lax
from jax.sharding import Mesh, PartitionSpec as P

FEATURE_WIDTH = 2048
FF = 7168
NY, NZ, NX, NCORE = 4, 8, 4, 2
ROWS = 64
TOK_DEV = 256
CAP_OLD = 70
CAP_NEW = 86
COLS = 896
QUART = COLS // NY
WIDE = 256
EDGE = 4
SENT = ROWS + 2 * EDGE

beta_one = 0.9
beta_two = 0.95
learn_rate = 0.01
decay_rate = 0.1
adam_eps = 1e-08
bias_one = 1.0 - 0.9**10
bias_two = 1.0 - 0.95**10

bf16 = jnp.bfloat16
f32 = jnp.float32
DP = ("y", "z")
MP = ("x", "core")


def ring(value, axis, by, size):
    return lax.ppermute(value, axis, [(i, (i + by) % size) for i in range(size)])


def wrapped(index, size):
    return lax.rem(index + size, jnp.int32(size))


def along_dp(value, by):
    peers = NY * NZ
    pairs = [(i, i + by) for i in range(peers) if 0 <= i + by < peers]
    return lax.ppermute(value, DP, pairs)


def rows_from(value, start, count, front, back):
    padding = [(front, back)] + [(0, 0)] * (value.ndim - 1)
    return lax.dynamic_slice_in_dim(jnp.pad(value, padding), front + start, count, axis=0)


def row_mask(condition):
    return condition[:, None, None]


def adam_step(master_rows, first_rows, second_rows, grads):
    first_new = beta_one * first_rows + (1.0 - beta_one) * grads
    second_new = beta_two * second_rows + (1.0 - beta_two) * grads * grads
    update = first_new / bias_one / (jnp.sqrt(second_new / bias_two) + adam_eps)
    master_new = master_rows - learn_rate * (update + decay_rate * master_rows)
    return (master_new, first_new, second_new)


def swap_along_y(pieces, y):
    def piece(step):
        return lax.dynamic_slice_in_dim(pieces, wrapped(y + step, NY), 1, axis=0)

    order = [piece(0)] + [ring(piece(step), "y", step, NY) for step in range(1, NY)]
    order = [order[0]] + order[:0:-1]
    return jnp.concatenate(
        [lax.select_n(wrapped(i - y, NY), *order) for i in range(NY)], axis=0
    )


def split_rows(master, shift, held):
    slots = jnp.arange(CAP_OLD, dtype=jnp.int32)
    own = jnp.where(row_mask(slots < held), master, 0.0).astype(bf16)
    rows = jnp.concatenate(
        [
            rows_from(own, -shift, ROWS, 16, 16),
            rows_from(own, -shift - EDGE, EDGE, 16, 16),
            rows_from(own, ROWS - shift, EDGE, 16, 16),
        ],
        axis=0,
    )
    split = rows.reshape(SENT, 3, NY, QUART)
    split = jnp.pad(split, ((0, 0), (0, 0), (0, 0), (0, WIDE - QUART)))
    return jnp.transpose(split, (2, 0, 1, 3)).reshape(NY, SENT, 3 * WIDE)


def gather_weights(own):
    blocks = {0: own}
    right, left = own, own
    for step in range(1, NZ // 2):
        right = ring(right, "z", 1, NZ)
        left = ring(left, "z", -1, NZ)
        blocks[-step] = right
        blocks[step] = left
    half = NY // 2
    far_low = ring(right[:half], "z", 1, NZ)
    far_high = ring(left[half:], "z", -1, NZ)
    blocks[NZ // 2] = jnp.concatenate([far_low, far_high], axis=0)
    return blocks


def joined(blocks, z):
    full = jnp.zeros((NY, NZ, SENT, 3 * WIDE), bf16)
    for step, block in blocks.items():
        full = lax.dynamic_update_slice_in_dim(full, block[:, None], wrapped(z + step, NZ), axis=1)
    full = full.reshape(NY * NZ, SENT, 3 * WIDE)
    none = jnp.zeros((1, EDGE, 3 * WIDE), bf16)
    before = jnp.concatenate([full[1:, ROWS : ROWS + EDGE], none], axis=0)
    behind = jnp.concatenate([none, full[:-1, ROWS + EDGE :]], axis=0)
    behind = jnp.pad(behind, ((0, 0), (0, ROWS - EDGE), (0, 0)))
    before = jnp.pad(before, ((0, 0), (ROWS - EDGE, 0), (0, 0)))
    return (full[:, :ROWS] + behind + before).reshape(FEATURE_WIDTH, 3 * WIDE)


def after(values, others):
    return lax.optimization_barrier((values, others))[0]


def gather_tokens(tokens, upstream, core, blocks):
    count = tokens.shape[0] // 2
    mine = jnp.stack(
        [lax.dynamic_slice_in_dim(v, core * count, count, axis=0) for v in (tokens, upstream)]
    )
    right = ring(mine, "y", 1, NY)
    left = ring(mine, "y", -1, NY)
    right, left = after((right, left), (blocks[2], blocks[-2]))
    half = count // 2
    far = jnp.concatenate(
        [ring(right[:, :half], "y", 1, NY), ring(left[:, half:], "y", -1, NY)], axis=1
    )
    groups = after(jnp.stack([left, far, right]), (blocks[3], blocks[-3]))
    other = ring(groups, "core", 1, NCORE)
    return tuple(
        jnp.concatenate([v] + [g[j, i] for g in (groups, other) for j in range(NY - 1)], axis=0)
        for i, v in enumerate((tokens, upstream))
    )


def in_order(rows, y, core):
    half = TOK_DEV // NCORE

    def part(at):
        return rows[TOK_DEV + at * half :][:half]

    groups = [rows[:TOK_DEV]]
    for j in range(NY - 1):
        mine, other = part(j), part(NY - 1 + j)
        pair = [jnp.where(core == 0, mine, other), jnp.where(core == 0, other, mine)]
        groups.append(jnp.concatenate(pair, axis=0))
    return jnp.concatenate(
        [lax.select_n(wrapped(i - y, NY), *groups) for i in range(NY)], axis=0
    )


def scatter_grads(terms, z, beside):
    terms = [v.reshape(NY, NZ, ROWS, -1) for v in terms]

    def block(step):
        at = wrapped(z + step, NZ)
        return jnp.concatenate(
            [lax.dynamic_slice_in_dim(v, at, 1, axis=1)[:, 0] for v in terms], axis=2
        )

    half = NY // 2

    def plus(a, b):
        return (a.astype(f32) + b.astype(f32)).astype(bf16)

    far = block(NZ // 2)
    right = ring(far[:half], "z", 1, NZ)
    left = ring(far[half:], "z", -1, NZ)
    up, down = block(NZ // 2 - 1), block(1 - NZ // 2)
    up = jnp.concatenate([plus(up[:half], right), up[half:]], axis=0)
    down = jnp.concatenate([down[:half], plus(down[half:], left)], axis=0)
    for step in range(NZ // 2 - 2, 0, -1):
        up = plus(block(step), ring(up, "z", 1, NZ))
        down = plus(block(-step), ring(down, "z", -1, NZ))
    up, down, beside = lax.optimization_barrier((up, down, beside))
    up, down = ring(up, "z", 1, NZ), ring(down, "z", -1, NZ)
    return (block(0).astype(f32) + up.astype(f32) + down.astype(f32)).astype(bf16), beside


def new_rows_of_grads(grads, new_start, p):
    block = along_dp(grads, 1)
    before = along_dp(grads[-EDGE:], 2)
    after = along_dp(grads[:EDGE], -1)
    window = jnp.concatenate([before, block, grads, after], axis=0)
    return rows_from(window, new_start - (ROWS * (p - 1) - EDGE), CAP_NEW, 0, 32)


def body(tokens, out_grad, master, moment_one, moment_two, old_offsets, new_offsets):
    y, z, core = lax.axis_index("y"), lax.axis_index("z"), lax.axis_index("core")
    p = y * NZ + z
    old_start = old_offsets[p]
    old_before = old_offsets[jnp.maximum(p - 1, 0)]
    new_start, new_end = new_offsets[p], new_offsets[p + 1]
    live = new_start != new_end
    scale_in = FEATURE_WIDTH ** (-0.5)
    scale_hidden = FF ** (-0.5)

    upstream = jnp.where(live, out_grad, jnp.zeros_like(out_grad))
    split = split_rows(master, old_start - ROWS * p, old_offsets[p + 1] - old_start)
    states = (master, moment_one, moment_two)
    first_left = along_dp(moment_one.astype(bf16), 1)
    split, first_left = lax.optimization_barrier((split, first_left))
    own = swap_along_y(split, y)
    tokens_in, upstream = after((tokens, upstream), own)
    blocks = gather_weights(own)
    tokens_all, upstream_all = gather_tokens(tokens_in, upstream, core, blocks)
    late = moment_two
    for k in (3, -3):
        blocks[k], late = lax.optimization_barrier((blocks[k], late))
    blocks[NZ // 2], later = lax.optimization_barrier((blocks[NZ // 2], master))
    second_left = along_dp(late.astype(bf16), 1)
    master_left = along_dp(later.astype(bf16), 1)
    weights = joined(blocks, z)

    def dot(a, b, contract=(1, 0)):
        return lax.dot_general(
            a, b, (((contract[0],), (contract[1],)), ((), ())), preferred_element_type=f32
        )

    gate_up = dot(tokens_all, weights[:, : 2 * WIDE]) * scale_in
    gate, up = gate_up[:, :WIDE], gate_up[:, WIDE:]
    down_weight = weights[:, 2 * WIDE :]
    back = dot(upstream_all, down_weight) * scale_hidden
    sigmoid = jax.nn.sigmoid(gate)
    hidden = (gate * sigmoid * up).astype(bf16)
    gate_grad = (back * up * sigmoid * (1.0 + gate * (1.0 - sigmoid))).astype(bf16)
    up_grad = (back * gate * sigmoid).astype(bf16)
    hidden, gate_grad, up_grad, second_left = lax.optimization_barrier(
        (hidden, gate_grad, up_grad, second_left)
    )
    partial = (dot(in_order(hidden, y, core), down_weight, (1, 1)) * scale_hidden).astype(bf16)
    both_grad = jnp.concatenate([gate_grad, up_grad], axis=1)
    top = (dot(tokens_all, both_grad, (0, 0)) * scale_in).astype(bf16)
    low = (dot(upstream_all, hidden, (0, 0)) * scale_hidden).astype(bf16)
    top, low, master_left = lax.optimization_barrier((top, low, master_left))
    from_left = (master_left, first_left, second_left)

    shared = lax.psum_scatter(partial, MP, scatter_dimension=1, tiled=True)
    slots = jnp.arange(CAP_NEW, dtype=jnp.int32)
    row = new_start + slots
    held = []
    for own_state, left in zip(states, from_left):
        moved = rows_from(left, new_start - old_before, CAP_NEW, 0, CAP_NEW).astype(f32)
        kept = rows_from(own_state, new_start - old_start, CAP_NEW, 72, 16)
        held.append(jnp.where(row_mask(row < old_start), moved, kept))

    summed, (held, shared) = scatter_grads((top, low), z, (held, shared))
    total = lax.psum_scatter(shared, "y", scatter_dimension=0, tiled=True)
    layer_output = jnp.where(live, total, jnp.zeros_like(total))
    quarters = swap_along_y(summed, y)
    quarters = quarters.reshape(NY, ROWS, 3, WIDE)[..., :QUART]
    grads = jnp.transpose(quarters, (1, 2, 0, 3)).reshape(ROWS, 3, COLS)
    grads = new_rows_of_grads(grads, new_start, p).astype(f32)

    updated = adam_step(*held, grads)
    in_range = row_mask(row < new_end)
    return tuple(jnp.where(in_range, v, 0.0) for v in updated) + (layer_output,)


def solution(mesh):
    grid = Mesh(mesh.devices.reshape(NY, NZ, NX, NCORE), DP + MP)
    state = P(DP, None, MP)
    return jax.shard_map(
        body,
        mesh=grid,
        in_specs=(P(DP, None), P(DP, None), state, state, state, P(), P()),
        out_specs=(state, state, state, P(DP, MP)),
        check_vma=False,
    )
```

```python
import jax
import jax.numpy as jnp
from jax import lax
from jax.sharding import Mesh, PartitionSpec as P

FEATURE_WIDTH = 2048
FF = 7168
NY, NZ, NX, NCORE = 4, 8, 4, 2
ROWS = 64
TOK_DEV = 256
CAP_OLD = 70
CAP_NEW = 86
COLS = 896
QUART = COLS // NY
WIDE = 256
EDGE = 4
SENT = ROWS + 2 * EDGE

beta_one = 0.9
beta_two = 0.95
learn_rate = 0.01
decay_rate = 0.1
adam_eps = 1e-08
bias_one = 1.0 - 0.9**10
bias_two = 1.0 - 0.95**10

bf16 = jnp.bfloat16
f32 = jnp.float32
DP = ("y", "z")
MP = ("x", "core")


def ring(value, axis, by, size):
    return lax.ppermute(value, axis, [(i, (i + by) % size) for i in range(size)])


def wrapped(index, size):
    return lax.rem(index + size, jnp.int32(size))


def along_dp(value, by):
    peers = NY * NZ
    pairs = [(i, i + by) for i in range(peers) if 0 <= i + by < peers]
    return lax.ppermute(value, DP, pairs)


def rows_from(value, start, count, front, back):
    padding = [(front, back)] + [(0, 0)] * (value.ndim - 1)
    return lax.dynamic_slice_in_dim(jnp.pad(value, padding), front + start, count, axis=0)


def row_mask(condition):
    return condition[:, None, None]


def adam_step(master_rows, first_rows, second_rows, grads):
    first_new = beta_one * first_rows + (1.0 - beta_one) * grads
    second_new = beta_two * second_rows + (1.0 - beta_two) * grads * grads
    update = first_new / bias_one / (jnp.sqrt(second_new / bias_two) + adam_eps)
    master_new = master_rows - learn_rate * (update + decay_rate * master_rows)
    return (master_new, first_new, second_new)


def swap_along_y(pieces, y):
    def piece(step):
        return lax.dynamic_slice_in_dim(pieces, wrapped(y + step, NY), 1, axis=0)

    order = [piece(0)] + [ring(piece(step), "y", step, NY) for step in range(1, NY)]
    order = [order[0]] + order[:0:-1]
    return jnp.concatenate(
        [lax.select_n(wrapped(i - y, NY), *order) for i in range(NY)], axis=0
    )


def split_rows(master, shift, held):
    slots = jnp.arange(CAP_OLD, dtype=jnp.int32)
    own = jnp.where(row_mask(slots < held), master, 0.0).astype(bf16)
    rows = jnp.concatenate(
        [
            rows_from(own, -shift, ROWS, 16, 16),
            rows_from(own, -shift - EDGE, EDGE, 16, 16),
            rows_from(own, ROWS - shift, EDGE, 16, 16),
        ],
        axis=0,
    )
    split = rows.reshape(SENT, 3, NY, QUART)
    split = jnp.pad(split, ((0, 0), (0, 0), (0, 0), (0, WIDE - QUART)))
    return jnp.transpose(split, (2, 0, 1, 3)).reshape(NY, SENT, 3 * WIDE)


def gather_weights(own):
    blocks = {0: own}
    right, left = own, own
    for step in range(1, NZ // 2):
        right = ring(right, "z", 1, NZ)
        left = ring(left, "z", -1, NZ)
        blocks[-step] = right
        blocks[step] = left
    half = NY // 2
    far_low = ring(right[:half], "z", 1, NZ)
    far_high = ring(left[half:], "z", -1, NZ)
    blocks[NZ // 2] = jnp.concatenate([far_low, far_high], axis=0)
    return blocks


def joined(blocks, z):
    full = jnp.zeros((NY, NZ, SENT, 3 * WIDE), bf16)
    for step, block in blocks.items():
        full = lax.dynamic_update_slice_in_dim(full, block[:, None], wrapped(z + step, NZ), axis=1)
    full = full.reshape(NY * NZ, SENT, 3 * WIDE)
    none = jnp.zeros((1, EDGE, 3 * WIDE), bf16)
    before = jnp.concatenate([full[1:, ROWS : ROWS + EDGE], none], axis=0)
    behind = jnp.concatenate([none, full[:-1, ROWS + EDGE :]], axis=0)
    behind = jnp.pad(behind, ((0, 0), (0, ROWS - EDGE), (0, 0)))
    before = jnp.pad(before, ((0, 0), (ROWS - EDGE, 0), (0, 0)))
    return (full[:, :ROWS] + behind + before).reshape(FEATURE_WIDTH, 3 * WIDE)


def after(values, others):
    return lax.optimization_barrier((values, others))[0]


def gather_tokens(tokens, upstream, core, blocks):
    count = tokens.shape[0] // 2
    mine = jnp.stack(
        [lax.dynamic_slice_in_dim(v, core * count, count, axis=0) for v in (tokens, upstream)]
    )
    right = ring(mine, "y", 1, NY)
    left = ring(mine, "y", -1, NY)
    right, left = after((right, left), (blocks[2], blocks[-2]))
    half = count // 2
    far = jnp.concatenate(
        [ring(right[:, :half], "y", 1, NY), ring(left[:, half:], "y", -1, NY)], axis=1
    )
    groups = after(jnp.stack([left, far, right]), (blocks[3], blocks[-3]))
    other = ring(groups, "core", 1, NCORE)
    return tuple(
        jnp.concatenate([v] + [g[j, i] for g in (groups, other) for j in range(NY - 1)], axis=0)
        for i, v in enumerate((tokens, upstream))
    )


def in_order(rows, y, core):
    half = TOK_DEV // NCORE

    def part(at):
        return rows[TOK_DEV + at * half :][:half]

    groups = [rows[:TOK_DEV]]
    for j in range(NY - 1):
        mine, other = part(j), part(NY - 1 + j)
        pair = [jnp.where(core == 0, mine, other), jnp.where(core == 0, other, mine)]
        groups.append(jnp.concatenate(pair, axis=0))
    return jnp.concatenate(
        [lax.select_n(wrapped(i - y, NY), *groups) for i in range(NY)], axis=0
    )


def scatter_grads(terms, z, arriving, beside):
    terms = [v.reshape(NY, NZ, ROWS, -1) for v in terms]

    def block(step):
        at = wrapped(z + step, NZ)
        return jnp.concatenate(
            [lax.dynamic_slice_in_dim(v, at, 1, axis=1)[:, 0] for v in terms], axis=2
        )

    half = NY // 2

    def plus(a, b):
        return (a.astype(f32) + b.astype(f32)).astype(bf16)

    far = block(NZ // 2)
    right = ring(far[:half], "z", 1, NZ)
    left = ring(far[half:], "z", -1, NZ)
    right, left, arriving = lax.optimization_barrier((right, left, arriving))
    up, down = block(NZ // 2 - 1), block(1 - NZ // 2)
    up = jnp.concatenate([plus(up[:half], right), up[half:]], axis=0)
    down = jnp.concatenate([down[:half], plus(down[half:], left)], axis=0)
    for step in range(NZ // 2 - 2, 0, -1):
        up = plus(block(step), ring(up, "z", 1, NZ))
        down = plus(block(-step), ring(down, "z", -1, NZ))
    up, down, beside = lax.optimization_barrier((up, down, beside(arriving)))
    up, down = ring(up, "z", 1, NZ), ring(down, "z", -1, NZ)
    return (block(0).astype(f32) + up.astype(f32) + down.astype(f32)).astype(bf16), beside


def new_rows_of_grads(grads, new_start, p):
    block = along_dp(grads, 1)
    before = along_dp(grads[-EDGE:], 2)
    after = along_dp(grads[:EDGE], -1)
    window = jnp.concatenate([before, block, grads, after], axis=0)
    return rows_from(window, new_start - (ROWS * (p - 1) - EDGE), CAP_NEW, 0, 32)


def body(tokens, out_grad, master, moment_one, moment_two, old_offsets, new_offsets):
    y, z, core = lax.axis_index("y"), lax.axis_index("z"), lax.axis_index("core")
    p = y * NZ + z
    old_start = old_offsets[p]
    old_before = old_offsets[jnp.maximum(p - 1, 0)]
    new_start, new_end = new_offsets[p], new_offsets[p + 1]
    live = new_start != new_end
    scale_in = FEATURE_WIDTH ** (-0.5)
    scale_hidden = FF ** (-0.5)

    upstream = jnp.where(live, out_grad, jnp.zeros_like(out_grad))
    split = split_rows(master, old_start - ROWS * p, old_offsets[p + 1] - old_start)
    states = (master, moment_one, moment_two)
    own = swap_along_y(split, y)
    tokens_in, upstream = after((tokens, upstream), own)
    blocks = gather_weights(own)
    tokens_all, upstream_all = gather_tokens(tokens_in, upstream, core, blocks)
    late, first_cast = moment_two, moment_one.astype(bf16)
    for k in (3, -3):
        blocks[k], late, first_cast = lax.optimization_barrier((blocks[k], late, first_cast))
    blocks[NZ // 2], later = lax.optimization_barrier((blocks[NZ // 2], master))
    second_left = along_dp(late.astype(bf16), 1)
    master_left = along_dp(later.astype(bf16), 1)
    weights = joined(blocks, z)

    def dot(a, b, contract=(1, 0)):
        return lax.dot_general(
            a, b, (((contract[0],), (contract[1],)), ((), ())), preferred_element_type=f32
        )

    gate_up = dot(tokens_all, weights[:, : 2 * WIDE]) * scale_in
    gate, up = gate_up[:, :WIDE], gate_up[:, WIDE:]
    down_weight = weights[:, 2 * WIDE :]
    back = dot(upstream_all, down_weight) * scale_hidden
    sigmoid = jax.nn.sigmoid(gate)
    hidden = (gate * sigmoid * up).astype(bf16)
    gate_grad = (back * up * sigmoid * (1.0 + gate * (1.0 - sigmoid))).astype(bf16)
    up_grad = (back * gate * sigmoid).astype(bf16)
    hidden, gate_grad, up_grad, second_left = lax.optimization_barrier(
        (hidden, gate_grad, up_grad, second_left)
    )
    partial = (dot(in_order(hidden, y, core), down_weight, (1, 1)) * scale_hidden).astype(bf16)
    both_grad = jnp.concatenate([gate_grad, up_grad], axis=1)
    top = (dot(tokens_all, both_grad, (0, 0)) * scale_in).astype(bf16)
    top, first_cast = lax.optimization_barrier((top, first_cast))
    first_left = along_dp(first_cast, 1)
    low = (dot(upstream_all, hidden, (0, 0)) * scale_hidden).astype(bf16)
    top, low, master_left = lax.optimization_barrier((top, low, master_left))

    shared = lax.psum_scatter(partial, MP, scatter_dimension=1, tiled=True)
    slots = jnp.arange(CAP_NEW, dtype=jnp.int32)
    row = new_start + slots

    def placed(own_state, left):
        moved = rows_from(left, new_start - old_before, CAP_NEW, 0, CAP_NEW).astype(f32)
        kept = rows_from(own_state, new_start - old_start, CAP_NEW, 72, 16)
        return jnp.where(row_mask(row < old_start), moved, kept)

    def beside(first_left):
        from_left = (master_left, first_left, second_left)
        return [placed(v, left) for v, left in zip(states, from_left)], shared

    summed, (held, shared) = scatter_grads((top, low), z, first_left, beside)
    total = lax.psum_scatter(shared, "y", scatter_dimension=0, tiled=True)
    layer_output = jnp.where(live, total, jnp.zeros_like(total))
    quarters = swap_along_y(summed, y)
    quarters = quarters.reshape(NY, ROWS, 3, WIDE)[..., :QUART]
    grads = jnp.transpose(quarters, (1, 2, 0, 3)).reshape(ROWS, 3, COLS)
    grads = new_rows_of_grads(grads, new_start, p).astype(f32)

    updated = adam_step(*held, grads)
    in_range = row_mask(row < new_end)
    return tuple(jnp.where(in_range, v, 0.0) for v in updated) + (layer_output,)


def solution(mesh):
    grid = Mesh(mesh.devices.reshape(NY, NZ, NX, NCORE), DP + MP)
    state = P(DP, None, MP)
    return jax.shard_map(
        body,
        mesh=grid,
        in_specs=(P(DP, None), P(DP, None), state, state, state, P(), P()),
        out_specs=(state, state, state, P(DP, MP)),
        check_vma=False,
    )
```

```python
import jax
import jax.numpy as jnp
from jax import lax
from jax.sharding import Mesh, PartitionSpec as P

FEATURE_WIDTH = 2048
FF = 7168
NY, NZ, NX, NCORE = 4, 8, 4, 2
ROWS = 64
TOK_DEV = 256
CAP_OLD = 70
CAP_NEW = 86
COLS = 896
QUART = COLS // NY
WIDE = 256
EDGE = 4
SENT = ROWS + 2 * EDGE

beta_one = 0.9
beta_two = 0.95
learn_rate = 0.01
decay_rate = 0.1
adam_eps = 1e-08
bias_one = 1.0 - 0.9**10
bias_two = 1.0 - 0.95**10

bf16 = jnp.bfloat16
f32 = jnp.float32
DP = ("y", "z")
MP = ("x", "core")


def ring(value, axis, by, size):
    return lax.ppermute(value, axis, [(i, (i + by) % size) for i in range(size)])


def wrapped(index, size):
    return lax.rem(index + size, jnp.int32(size))


def along_dp(value, by):
    peers = NY * NZ
    pairs = [(i, i + by) for i in range(peers) if 0 <= i + by < peers]
    return lax.ppermute(value, DP, pairs)


def rows_from(value, start, count, front, back):
    padding = [(front, back)] + [(0, 0)] * (value.ndim - 1)
    return lax.dynamic_slice_in_dim(jnp.pad(value, padding), front + start, count, axis=0)


def row_mask(condition):
    return condition[:, None, None]


def adam_step(master_rows, first_rows, second_rows, grads):
    first_new = beta_one * first_rows + (1.0 - beta_one) * grads
    second_new = beta_two * second_rows + (1.0 - beta_two) * grads * grads
    update = first_new / bias_one / (jnp.sqrt(second_new / bias_two) + adam_eps)
    master_new = master_rows - learn_rate * (update + decay_rate * master_rows)
    return (master_new, first_new, second_new)


def swap_along_y(pieces, y):
    def piece(step):
        return lax.dynamic_slice_in_dim(pieces, wrapped(y + step, NY), 1, axis=0)

    order = [piece(0)] + [ring(piece(step), "y", step, NY) for step in range(1, NY)]
    order = [order[0]] + order[:0:-1]
    return jnp.concatenate(
        [lax.select_n(wrapped(i - y, NY), *order) for i in range(NY)], axis=0
    )


def split_rows(master, shift, held):
    slots = jnp.arange(CAP_OLD, dtype=jnp.int32)
    own = jnp.where(row_mask(slots < held), master, 0.0).astype(bf16)
    rows = jnp.concatenate(
        [
            rows_from(own, -shift, ROWS, 16, 16),
            rows_from(own, -shift - EDGE, EDGE, 16, 16),
            rows_from(own, ROWS - shift, EDGE, 16, 16),
        ],
        axis=0,
    )
    split = rows.reshape(SENT, 3, NY, QUART)
    split = jnp.pad(split, ((0, 0), (0, 0), (0, 0), (0, WIDE - QUART)))
    return jnp.transpose(split, (2, 0, 1, 3)).reshape(NY, SENT, 3 * WIDE)


def gather_weights(own):
    blocks = {0: own}
    right, left = own, own
    for step in range(1, NZ // 2):
        right = ring(right, "z", 1, NZ)
        left = ring(left, "z", -1, NZ)
        blocks[-step] = right
        blocks[step] = left
    half = NY // 2
    far_low = ring(right[:half], "z", 1, NZ)
    far_high = ring(left[half:], "z", -1, NZ)
    blocks[NZ // 2] = jnp.concatenate([far_low, far_high], axis=0)
    return blocks


def joined(blocks, z):
    full = jnp.zeros((NY, NZ, SENT, 3 * WIDE), bf16)
    for step, block in blocks.items():
        full = lax.dynamic_update_slice_in_dim(full, block[:, None], wrapped(z + step, NZ), axis=1)
    full = full.reshape(NY * NZ, SENT, 3 * WIDE)
    none = jnp.zeros((1, EDGE, 3 * WIDE), bf16)
    before = jnp.concatenate([full[1:, ROWS : ROWS + EDGE], none], axis=0)
    behind = jnp.concatenate([none, full[:-1, ROWS + EDGE :]], axis=0)
    behind = jnp.pad(behind, ((0, 0), (0, ROWS - EDGE), (0, 0)))
    before = jnp.pad(before, ((0, 0), (ROWS - EDGE, 0), (0, 0)))
    return (full[:, :ROWS] + behind + before).reshape(FEATURE_WIDTH, 3 * WIDE)


def after(values, others):
    return lax.optimization_barrier((values, others))[0]


def gather_tokens(tokens, upstream, core, blocks):
    count = tokens.shape[0] // 2
    mine = jnp.stack(
        [lax.dynamic_slice_in_dim(v, core * count, count, axis=0) for v in (tokens, upstream)]
    )
    right = ring(mine, "y", 1, NY)
    left = ring(mine, "y", -1, NY)
    right, left = after((right, left), (blocks[2], blocks[-2]))
    half = count // 2
    far = jnp.concatenate(
        [ring(right[:, :half], "y", 1, NY), ring(left[:, half:], "y", -1, NY)], axis=1
    )
    groups = after(jnp.stack([left, far, right]), (blocks[3], blocks[-3]))
    other = ring(groups, "core", 1, NCORE)
    return tuple(
        jnp.concatenate([v] + [g[j, i] for g in (groups, other) for j in range(NY - 1)], axis=0)
        for i, v in enumerate((tokens, upstream))
    )


def in_order(rows, y, core):
    half = TOK_DEV // NCORE

    def part(at):
        return rows[TOK_DEV + at * half :][:half]

    groups = [rows[:TOK_DEV]]
    for j in range(NY - 1):
        mine, other = part(j), part(NY - 1 + j)
        pair = [jnp.where(core == 0, mine, other), jnp.where(core == 0, other, mine)]
        groups.append(jnp.concatenate(pair, axis=0))
    return jnp.concatenate(
        [lax.select_n(wrapped(i - y, NY), *groups) for i in range(NY)], axis=0
    )


def scatter_grads(terms, z, beside):
    terms = [v.reshape(NY, NZ, ROWS, -1) for v in terms]

    def block(step):
        at = wrapped(z + step, NZ)
        return jnp.concatenate(
            [lax.dynamic_slice_in_dim(v, at, 1, axis=1)[:, 0] for v in terms], axis=2
        )

    half = NY // 2

    def plus(a, b):
        return (a.astype(f32) + b.astype(f32)).astype(bf16)

    far = block(NZ // 2)
    right = ring(far[:half], "z", 1, NZ)
    left = ring(far[half:], "z", -1, NZ)
    up, down = block(NZ // 2 - 1), block(1 - NZ // 2)
    up = jnp.concatenate([plus(up[:half], right), up[half:]], axis=0)
    down = jnp.concatenate([down[:half], plus(down[half:], left)], axis=0)
    for step in range(NZ // 2 - 2, 0, -1):
        up = plus(block(step), ring(up, "z", 1, NZ))
        down = plus(block(-step), ring(down, "z", -1, NZ))
    up, down, beside = lax.optimization_barrier((up, down, beside))
    up, down = ring(up, "z", 1, NZ), ring(down, "z", -1, NZ)
    return (block(0).astype(f32) + up.astype(f32) + down.astype(f32)).astype(bf16), beside


def new_rows_of_grads(grads, new_start, p):
    block = along_dp(grads, 1)
    before = along_dp(grads[-EDGE:], 2)
    after = along_dp(grads[:EDGE], -1)
    window = jnp.concatenate([before, block, grads, after], axis=0)
    return rows_from(window, new_start - (ROWS * (p - 1) - EDGE), CAP_NEW, 0, 32)


def body(tokens, out_grad, master, moment_one, moment_two, old_offsets, new_offsets):
    y, z, core = lax.axis_index("y"), lax.axis_index("z"), lax.axis_index("core")
    p = y * NZ + z
    old_start = old_offsets[p]
    old_before = old_offsets[jnp.maximum(p - 1, 0)]
    new_start, new_end = new_offsets[p], new_offsets[p + 1]
    live = new_start != new_end
    scale_in = FEATURE_WIDTH ** (-0.5)
    scale_hidden = FF ** (-0.5)

    upstream = jnp.where(live, out_grad, jnp.zeros_like(out_grad))
    split = split_rows(master, old_start - ROWS * p, old_offsets[p + 1] - old_start)
    states = (master, moment_one, moment_two)
    own = swap_along_y(split, y)
    tokens_in, upstream = after((tokens, upstream), own)
    blocks = gather_weights(own)
    tokens_all, upstream_all = gather_tokens(tokens_in, upstream, core, blocks)
    late = (moment_one, moment_two)
    for k in (3, -3):
        blocks[k], late = lax.optimization_barrier((blocks[k], late))
    blocks[NZ // 2], later = lax.optimization_barrier((blocks[NZ // 2], master))
    spare = ((0, SENT - CAP_OLD), (0, 0), (0, 0))
    moments_left = along_dp(
        jnp.concatenate([jnp.pad(v.astype(bf16), spare) for v in late], axis=0), 1
    )
    master_left = along_dp(later.astype(bf16), 1)
    weights = joined(blocks, z)

    def dot(a, b, contract=(1, 0)):
        return lax.dot_general(
            a, b, (((contract[0],), (contract[1],)), ((), ())), preferred_element_type=f32
        )

    gate_up = dot(tokens_all, weights[:, : 2 * WIDE]) * scale_in
    gate, up = gate_up[:, :WIDE], gate_up[:, WIDE:]
    down_weight = weights[:, 2 * WIDE :]
    back = dot(upstream_all, down_weight) * scale_hidden
    sigmoid = jax.nn.sigmoid(gate)
    hidden = (gate * sigmoid * up).astype(bf16)
    gate_grad = (back * up * sigmoid * (1.0 + gate * (1.0 - sigmoid))).astype(bf16)
    up_grad = (back * gate * sigmoid).astype(bf16)
    hidden, gate_grad, up_grad, moments_left = lax.optimization_barrier(
        (hidden, gate_grad, up_grad, moments_left)
    )
    partial = (dot(in_order(hidden, y, core), down_weight, (1, 1)) * scale_hidden).astype(bf16)
    both_grad = jnp.concatenate([gate_grad, up_grad], axis=1)
    top = (dot(tokens_all, both_grad, (0, 0)) * scale_in).astype(bf16)
    low = (dot(upstream_all, hidden, (0, 0)) * scale_hidden).astype(bf16)
    top, low, master_left = lax.optimization_barrier((top, low, master_left))
    from_left = (master_left, moments_left[:CAP_OLD], moments_left[SENT:][:CAP_OLD])

    shared = lax.psum_scatter(partial, MP, scatter_dimension=1, tiled=True)
    slots = jnp.arange(CAP_NEW, dtype=jnp.int32)
    row = new_start + slots
    held = []
    for own_state, left in zip(states, from_left):
        moved = rows_from(left, new_start - old_before, CAP_NEW, 0, CAP_NEW).astype(f32)
        kept = rows_from(own_state, new_start - old_start, CAP_NEW, 72, 16)
        held.append(jnp.where(row_mask(row < old_start), moved, kept))

    summed, (held, shared) = scatter_grads((top, low), z, (held, shared))
    total = lax.psum_scatter(shared, "y", scatter_dimension=0, tiled=True)
    layer_output = jnp.where(live, total, jnp.zeros_like(total))
    quarters = swap_along_y(summed, y)
    quarters = quarters.reshape(NY, ROWS, 3, WIDE)[..., :QUART]
    grads = jnp.transpose(quarters, (1, 2, 0, 3)).reshape(ROWS, 3, COLS)
    grads = new_rows_of_grads(grads, new_start, p).astype(f32)

    updated = adam_step(*held, grads)
    in_range = row_mask(row < new_end)
    return tuple(jnp.where(in_range, v, 0.0) for v in updated) + (layer_output,)


def solution(mesh):
    grid = Mesh(mesh.devices.reshape(NY, NZ, NX, NCORE), DP + MP)
    state = P(DP, None, MP)
    return jax.shard_map(
        body,
        mesh=grid,
        in_specs=(P(DP, None), P(DP, None), state, state, state, P(), P()),
        out_specs=(state, state, state, P(DP, MP)),
        check_vma=False,
    )
```
